128 devices in a mesh: grp: 4 (over y), seq: 32 (over x, z, core).
Axes of the slice: x: 4, y: 4, z: 4, core: 2. Of those that a mesh axis runs over, the one named last changes fastest.
Arguments:
- cand_x: bfloat16 [32768, 1024], P(('grp', 'seq')), may hold values from -6 to 6
- w_in: bfloat16 [1024, 4096], replicated, may hold values from -0.1875 to 0.1875
- w_out: bfloat16 [1024, 1024], P('grp'), may hold values from -0.1875 to 0.1875
- hist_keys: bfloat16 [4, 8192, 1024], P('grp', 'seq'), may hold values from -9 to 9
- hist_values: bfloat16 [4, 8192, 1024], P('grp', 'seq'), may hold values from -0.29882812 to 0.29882812
- hist_len: int32 [4], P('grp'), may hold values from 1024 to 8192, as said below
- cand_count: int32 [4], P('grp'), may hold values from 1024 to 8192, as said below
- panel_map: int32 [1024], P(('grp', 'seq')), may hold values from 0 to 255, as said below
Outputs:
- scored: bfloat16 [32768, 1024], P(('grp', 'seq'))
The draws below stay inside these ranges and needn't reach their ends.
Inputs may be any that keep to these rules, and one draw needn't show every extreme that they name: `hist_len`: each user's lengths count its first events; one user has exactly 8192. `cand_count`: each user's real candidates are its candidate numbers below the count; one user has exactly 8192. `panel_map`: for each user, the 256 entries on the 32 devices of its group name every panel number once.
All inputs are finite; a program needn't handle non-finite values.
Results may differ from the reference program's by a relative error of at most 0.0055.
Values may be sent and summed in bfloat16 or wider, within the bound.
A program may use at most 192 MiB of HBM per device.

```python
import jax
import jax.numpy as jnp
from jax import lax

D = 1024
HEADS = 8
PANEL = 32
USERS = 4
PANELS = 256
CANDS = 8192
HIST = 8192


def draw_hist_len(key, part):
    key = jax.random.fold_in(key, 1)
    first, second = jax.random.split(key)
    base = jax.random.randint(first, (USERS,), HIST // 8, HIST + 1)
    which = jax.random.randint(second, (), 0, USERS)
    return base.at[which].set(HIST).astype(jnp.int32)


def draw_cand_count(key, part):
    key = jax.random.fold_in(key, 2)
    first, second = jax.random.split(key)
    base = jax.random.randint(first, (USERS,), CANDS // 8, CANDS + 1)
    which = jax.random.randint(second, (), 0, USERS)
    return base.at[which].set(CANDS).astype(jnp.int32)


def draw_panel_map(key, part):
    key = jax.random.fold_in(key, 3)
    user_keys = jax.random.split(key, USERS)
    orders = jax.vmap(lambda k: jax.random.permutation(k, PANELS))(user_keys)
    return orders.reshape(USERS * PANELS).astype(jnp.int32)


def levels(own_key, shape, cuts, smallest, largest):
    def one(dim, parts):
        steps = jax.random.uniform(jax.random.fold_in(jax.random.fold_in(own_key, 6), dim), (parts,), jnp.float32, smallest / len(cuts), largest / len(cuts))
        return jnp.repeat(jnp.exp(steps), shape[dim] // parts).reshape((-1,) + (1,) * (len(shape) - dim - 1))

    loudness = one(*cuts[0])
    for cut in cuts[1:]:
        loudness = loudness * one(*cut)
    return loudness


def scatter_about(key, shape, spread, limit, cuts=(), held_as=jnp.bfloat16):
    level = levels(key, shape, cuts, -0.22, 0.18) if cuts else 1.0
    result = jax.random.normal(key, shape, jnp.float32) * spread * level
    return jnp.minimum(jnp.maximum(result, -limit), limit).astype(held_as)


def setup_inputs(seed: int = 0) -> dict:
    splits = jax.random.split(jax.random.key(seed), 9)
    return {
        "cand_x": scatter_about(splits[0], (USERS * CANDS, D), 1.0, 6.0, ((0, 128),)),
        "w_in": scatter_about(splits[1], (D, 4 * D), D ** -0.5, 0.1875),
        "w_out": scatter_about(splits[2], (D, D), D ** -0.5, 0.1875, ((0, 4),)),
        "hist_keys": scatter_about(splits[3], (USERS, HIST, D), 1.5, 9.0, ((0, 4), (1, 32))),
        "hist_values": scatter_about(splits[4], (USERS, HIST, D), 0.05, 0.29882812, ((0, 4), (1, 32))),
        "hist_len": draw_hist_len(jax.random.fold_in(splits[8], 71), 0),
        "cand_count": draw_cand_count(jax.random.fold_in(splits[8], 71), 0),
        "panel_map": draw_panel_map(jax.random.fold_in(splits[8], 71), 0),
    }


eps = 1e-06

def layer_norm(x):
    mean = lax.optimization_barrier(jnp.mean(x, axis=-1, keepdims=True))
    var = lax.optimization_barrier(jnp.mean((x - mean) ** 2, axis=-1, keepdims=True))
    return (x - mean) / jnp.sqrt(var + eps)

def reference(cand_x, w_in, w_out, hist_keys, hist_values, hist_len, cand_count, panel_map):
    width = cand_x.shape[1]
    head = width // HEADS
    scale = 1.0 / jnp.sqrt(jnp.float32(head))
    x32 = cand_x.astype(jnp.float32)
    normed = layer_norm(x32).astype(jnp.bfloat16)
    proj = jax.nn.silu(jnp.dot(normed, w_in, preferred_element_type=jnp.float32)).astype(jnp.bfloat16)
    u_part = proj[:, 0:width]
    v_part = proj[:, width:2 * width]
    q_part = proj[:, 2 * width:3 * width]
    k_part = proj[:, 3 * width:4 * width]
    total = cand_x.shape[0]
    q_heads = q_part.astype(jnp.float32).reshape(total, HEADS, head)
    k_heads = k_part.astype(jnp.float32).reshape(total, HEADS, head)
    v_heads = v_part.astype(jnp.float32).reshape(total, HEADS, head)
    self_w = jax.nn.silu(lax.optimization_barrier(jnp.sum(q_heads * k_heads, axis=-1)) * scale).astype(jnp.bfloat16)
    self_term = (self_w.astype(jnp.float32)[:, :, None] * v_heads).reshape(total, width)
    block = 512 if CANDS % 512 == 0 else CANDS
    q_users = q_part.reshape(USERS, CANDS // block, block, HEADS, head)
    positions = jnp.arange(HIST, dtype=jnp.int32)

    def per_user(packed):
        queries, keys, values, length = packed
        keys32 = keys.astype(jnp.float32).reshape(HIST, HEADS, head)
        values32 = values.astype(jnp.float32).reshape(HIST, HEADS, head)
        keep = positions < length

        def per_block(qblock):
            scores = jnp.einsum('rhd,nhd->hrn', qblock.astype(jnp.float32), keys32) * scale
            weights = jnp.where(keep[None, None, :], jax.nn.silu(scores), 0.0).astype(jnp.bfloat16)
            return jnp.einsum('hrn,nhd->rhd', weights.astype(jnp.float32), values32).reshape(block, width)
        return lax.map(per_block, queries)
    hist_term = lax.map(per_user, (q_users, hist_keys, hist_values, hist_len)).reshape(total, width)
    attn = hist_term + self_term
    gated = (layer_norm(attn) * u_part.astype(jnp.float32)).astype(jnp.bfloat16)
    mixed = x32 + jnp.dot(gated, w_out, preferred_element_type=jnp.float32)
    cand_index = (panel_map.reshape(USERS, PANELS)[:, :, None] * PANEL + jnp.arange(PANEL, dtype=jnp.int32)[None, None, :]).reshape(USERS, CANDS)
    valid = (cand_index < cand_count[:, None]).reshape(total)
    return jnp.where(valid[:, None], mixed, 0.0).astype(jnp.bfloat16)
```

```python
import jax
import jax.numpy as jnp
from jax import lax
from jax.experimental import pallas as pl
from jax.experimental.pallas import tpu as pltpu
from jax.sharding import PartitionSpec as P

MESH = pl.DeviceIdType.MESH
HEADS = 8
PANEL = 32
ROWS = 256
D = 1024
HD = 128
eps = 1e-06
SCALE = HD**-0.5
NT = (((1,), (1,)), ((), ()))
BF = jnp.bfloat16
F32 = jnp.float32


def silu(z):
    h = z * 0.5
    return h + h * jnp.tanh(h)


def weight(s):
    h = (s * (0.5 * SCALE)).astype(BF)
    return h + h * jnp.tanh(h)


def layer_norm(x):
    mean = jnp.mean(x, axis=-1, keepdims=True)
    var = jnp.mean((x - mean) ** 2, axis=-1, keepdims=True)
    return (x - mean) / jnp.sqrt(var + eps)


def kernel(
    x_hbm,
    win_hbm,
    wout_hbm,
    hk_hbm,
    hv_hbm,
    hlen_ref,
    cnt_ref,
    pmap_ref,
    out_ref,
    x_v,
    n_v,
    win_v,
    hv_v,
    q_own,
    k_own,
    v_own,
    u_own,
    self_v,
    k_all,
    v_all,
    q_all,
    acc,
    osend,
    orecv,
    asend,
    attn_v,
    wout_v,
    loc,
    k_snd,
    k_rcv,
    v_snd,
    v_rcv,
    q_snd,
    q_rcv,
    o_snd,
    o_rcv,
    a_snd,
    a_rcv,
    w_snd,
    w_rcv,
):
    g = lax.axis_index("grp")
    s = lax.axis_index("seq")
    x, z, c = s // 8, (s // 2) % 4, s % 2
    xb, zb = x // 2, z // 2
    xh, zh = x + xb * (3 - 2 * x), z + zb * (3 - 2 * z)
    head = xh * 4 + zh * 2 + c

    def seq_of(x_, z_, c_):
        return x_ * 8 + z_ * 2 + c_

    def peer(d):
        d2, d1, d0 = d // 4, (d // 2) % 2, d % 2
        xp = xh + d2 * (1 - 2 * xh)
        zp = zh + d1 * (1 - 2 * zh)
        cp = c + d0 * (1 - 2 * c)
        return (g, seq_of(xp + xb * (3 - 2 * xp), zp + zb * (3 - 2 * zp), cp)), xp * 4 + zp * 2 + cp

    row_partner = (g, seq_of(x + (1 - c) * (3 - 2 * x), z + c * (3 - 2 * z), c))
    event_partner = (g, seq_of(x + c * (3 - 2 * x), z + (1 - c) * (3 - 2 * z), c))

    def cols(h):
        return pl.ds(pl.multiple_of(h * HD, HD), HD)

    def slot(d, n=1):
        return pl.ds(pl.multiple_of(d * ROWS, ROWS), n * ROWS)

    def remote(src, dst, snd, rcv, dev):
        return pltpu.make_async_remote_copy(
            src_ref=src, dst_ref=dst, send_sem=snd, recv_sem=rcv, device_id=dev, device_id_type=MESH
        )

    barrier = pltpu.get_barrier_semaphore()
    partners = [peer(d)[0] for d in range(1, 8)] + [row_partner, event_partner]
    partners += [((g + d) % 4, s) for d in range(1, 4)]
    for dev in partners:
        pl.semaphore_signal(barrier, inc=1, device_id=dev, device_id_type=MESH)

    ld_v = pltpu.make_async_copy(hv_hbm.at[0], hv_v, loc.at[0])
    ld_x = pltpu.make_async_copy(x_hbm, x_v, loc.at[1])
    ld_v.start()
    ld_x.start()
    ld_w = []
    for i, part in enumerate((2, 3, 1, 0)):
        cp = pltpu.make_async_copy(win_hbm.at[:, pl.ds(part * D, D)], win_v.at[part], loc.at[2 + i])
        cp.start()
        ld_w.append(cp)
    ld_wo = pltpu.make_async_copy(wout_hbm, wout_v.at[slot(g)], loc.at[6])
    ld_wo.start()
    own_k = pltpu.make_async_copy(hk_hbm.at[0, :, cols(head)], k_all.at[slot(0)], loc.at[7])
    own_k.start()

    ld_v.wait()
    pos = s * ROWS + lax.broadcasted_iota(jnp.int32, (ROWS, D), 0)
    hv_v[...] = jnp.where(pos < hlen_ref[0], hv_v[...].astype(F32), 0.0).astype(BF)

    pl.semaphore_wait(barrier, len(partners))

    sends = []

    def go(cp):
        cp.start()
        sends.append(cp)

    for d in range(1, 8):
        dev, h = peer(d)
        go(remote(hk_hbm.at[0, :, cols(h)], k_all.at[slot(d)], k_snd.at[d], k_rcv.at[d], dev))
    for d in range(1, 8):
        dev, h = peer(d)
        go(remote(hv_v.at[:, cols(h)], v_all.at[slot(d)], v_snd.at[d], v_rcv.at[d], dev))
    half = pl.ds(pl.multiple_of(c * 128, 128), 128)
    for d in range(1, 4):
        dst = wout_v.at[pl.ds(pl.multiple_of(g * 256 + c * 128, 128), 128)]
        go(remote(wout_hbm.at[half], dst, w_snd.at[d], w_rcv.at[d], ((g + d) % 4, s)))
    v_all[slot(0), :] = hv_v[:, cols(head)]

    ld_x.wait()
    n_v[...] = layer_norm(x_v[...].astype(F32)).astype(BF)

    def project(part, dst, lo, n):
        def piece(p, _):
            ds = pl.ds(pl.multiple_of(p * 256, 256), 256)
            dst[:, ds] = silu(jnp.dot(n_v[...], win_v[part, :, ds], preferred_element_type=F32)).astype(BF)
            return 0

        lax.fori_loop(lo, lo + n, piece, 0)

    ld_w[0].wait()
    project(2, q_own, 0, 4)
    for d in range(1, 8):
        dev, h = peer(d)
        go(remote(q_own.at[:, cols(h)], q_all.at[slot(d)], q_snd.at[d], q_rcv.at[d], dev))
    q_all[slot(0), :] = q_own[:, cols(head)]

    def arrived(buf, rcv, d):
        remote(buf.at[slot(d)], buf.at[slot(d)], rcv.at[d], rcv.at[d], event_partner).wait_recv()

    own_k.wait()
    work = [(3, k_own, i) for i in range(4)] + [(1, v_own, i) for i in range(4)] + [(0, u_own, i) for i in range(4)]
    done = 0
    for d in range(8):
        if d:
            arrived(k_all, k_rcv, d)
        go(remote(k_all.at[slot(d)], k_all.at[slot(8 + d)], k_snd.at[8 + d], k_rcv.at[8 + d], event_partner))
        if d:
            arrived(v_all, v_rcv, d)
        go(remote(v_all.at[slot(d)], v_all.at[slot(8 + d)], v_snd.at[8 + d], v_rcv.at[8 + d], event_partner))
        if d % 2 == 0:
            if d // 2 < 3:
                part, dst, _ = work[done]
                ld_w[1 + d // 2].wait()
                project(part, dst, 0, 4)
                done += 4
    for d in range(8):
        if d:
            arrived(q_all, q_rcv, d)
        go(remote(q_all.at[slot(d)], q_all.at[slot(8 + d)], q_snd.at[8 + d], q_rcv.at[8 + d], row_partner))

    for h in range(HEADS):
        ds = pl.ds(h * HD, HD)
        dot = jnp.sum(q_own[:, ds].astype(F32) * k_own[:, ds].astype(F32), axis=-1, keepdims=True)
        self_v[:, ds] = silu(dot * SCALE).astype(BF).astype(F32) * v_own[:, ds].astype(F32)

    def attend(rows, events):
        sc = lax.dot_general(q_all[rows, :], k_all[events, :], NT, preferred_element_type=F32)
        return jnp.dot(weight(sc), v_all[events, :], preferred_element_type=F32)

    def own_block(i, _):
        rows = slot(2 * i, 2)
        acc[rows, :] = attend(rows, pl.ds(0, 8 * ROWS))
        return 0

    lax.fori_loop(0, 4, own_block, 0)

    for d in range(1, 4):
        rows = pl.ds(pl.multiple_of(((g - d + 4) % 4) * 256 + c * 128, 128), 128)
        remote(wout_v.at[rows], wout_v.at[rows], w_rcv.at[d], w_rcv.at[d], event_partner).wait_recv()
        go(remote(wout_v.at[rows], wout_v.at[rows], w_snd.at[4 + d], w_rcv.at[4 + d], peer(1)[0]))

    for d in range(8, 16):
        arrived(k_all, k_rcv, d)
        arrived(v_all, v_rcv, d)
        arrived(q_all, q_rcv, d)

    def o_copy(i):
        return remote(osend.at[slot(2 * i, 2)], orecv.at[slot(2 * i, 2)], o_snd.at[i], o_rcv.at[i], row_partner)

    def partner_rows(n, _):
        i = 3 - n
        osend[slot(2 * i, 2), :] = attend(slot(8 + 2 * i, 2), pl.ds(0, 16 * ROWS)).astype(BF)
        o_copy(i).start()
        return 0

    lax.fori_loop(0, 4, partner_rows, 0)

    def a_copy(d):
        return remote(asend.at[slot(d)], attn_v.at[:, cols(head)], a_snd.at[d], a_rcv.at[d], peer(d)[0])

    def own_rows(n, _):
        i = 3 - n
        rows = slot(2 * i, 2)
        part = acc[rows, :] + attend(rows, pl.ds(8 * ROWS, 8 * ROWS))
        o_copy(i).wait_recv()
        asend[rows, :] = (part + orecv[rows, :].astype(F32)).astype(BF)
        a_copy(2 * i + 1).start()

        @pl.when(i > 0)
        def _():
            a_copy(2 * i).start()

        return 0

    lax.fori_loop(0, 4, own_rows, 0)
    attn_v[:, cols(head)] = asend[slot(0), :]

    for d in range(1, 4):
        rows = pl.ds(pl.multiple_of(((g - d + 4) % 4) * 256 + (1 - c) * 128, 128), 128)
        remote(wout_v.at[rows], wout_v.at[rows], w_rcv.at[4 + d], w_rcv.at[4 + d], event_partner).wait_recv()
    ld_wo.wait()
    for d in range(1, 8):
        h = peer(d)[1]
        remote(asend.at[slot(d)], attn_v.at[:, cols(h)], a_snd.at[d], a_rcv.at[d], event_partner).wait_recv()

    n_v[...] = (
        layer_norm(attn_v[...].astype(F32) + self_v[...]) * u_own[...].astype(F32)
    ).astype(BF)

    def out_piece(p, _):
        ds = pl.ds(pl.multiple_of(p * 256, 256), 256)
        mixed = x_v[:, ds].astype(F32) + jnp.dot(n_v[...], wout_v[:, ds], preferred_element_type=F32)
        for i in range(ROWS // PANEL):
            number = pmap_ref[i] * PANEL + lax.broadcasted_iota(jnp.int32, (PANEL, 256), 0)
            keep = mixed[i * PANEL : (i + 1) * PANEL]
            out_ref[pl.ds(i * PANEL, PANEL), ds] = jnp.where(number < cnt_ref[0], keep, 0.0).astype(BF)
        return 0

    lax.fori_loop(0, 4, out_piece, 0)

    for cp in sends:
        cp.wait_send()
    for i in range(4):
        o_copy(i).wait_send()
    for d in range(1, 8):
        a_copy(d).wait_send()


def per_device(cand_x, w_in, w_out, hist_keys, hist_values, hist_len, cand_count, panel_map):
    hbm = pl.BlockSpec(memory_space=pl.ANY)
    smem = pl.BlockSpec(memory_space=pltpu.SMEM)
    dma = pltpu.SemaphoreType.DMA
    return pl.pallas_call(
        kernel,
        out_shape=jax.ShapeDtypeStruct((ROWS, D), BF),
        in_specs=[hbm] * 5 + [smem] * 3,
        out_specs=pl.BlockSpec(memory_space=pltpu.VMEM),
        scratch_shapes=[
            pltpu.VMEM((ROWS, D), BF),
            pltpu.VMEM((ROWS, D), BF),
            pltpu.VMEM((4, D, D), BF),
            pltpu.VMEM((ROWS, D), BF),
            pltpu.VMEM((ROWS, D), BF),
            pltpu.VMEM((ROWS, D), BF),
            pltpu.VMEM((ROWS, D), BF),
            pltpu.VMEM((ROWS, D), BF),
            pltpu.VMEM((ROWS, D), F32),
            pltpu.VMEM((16 * ROWS, HD), BF),
            pltpu.VMEM((16 * ROWS, HD), BF),
            pltpu.VMEM((16 * ROWS, HD), BF),
            pltpu.VMEM((8 * ROWS, HD), F32),
            pltpu.VMEM((8 * ROWS, HD), BF),
            pltpu.VMEM((8 * ROWS, HD), BF),
            pltpu.VMEM((8 * ROWS, HD), BF),
            pltpu.VMEM((ROWS, D), BF),
            pltpu.VMEM((D, D), BF),
            dma((8,)),
            dma((16,)),
            dma((16,)),
            dma((16,)),
            dma((16,)),
            dma((16,)),
            dma((16,)),
            dma((4,)),
            dma((4,)),
            dma((8,)),
            dma((8,)),
            dma((8,)),
            dma((8,)),
        ],
        compiler_params=pltpu.CompilerParams(
            collective_id=0, has_side_effects=True, vmem_limit_bytes=56 * 2**20
        ),
    )(cand_x, w_in, w_out, hist_keys, hist_values, hist_len, cand_count, panel_map)


def solution(mesh):
    return jax.shard_map(
        per_device,
        mesh=mesh,
        in_specs=(
            P(("grp", "seq"), None),
            P(),
            P("grp", None),
            P("grp", "seq", None),
            P("grp", "seq", None),
            P("grp"),
            P("grp"),
            P(("grp", "seq")),
        ),
        out_specs=P(("grp", "seq"), None),
        check_vma=False,
    )
```

```python
import jax
import jax.numpy as jnp
from jax import lax
from jax.experimental import pallas as pl
from jax.experimental.pallas import tpu as pltpu
from jax.sharding import PartitionSpec as P

MESH = pl.DeviceIdType.MESH
HEADS = 8
PANEL = 32
ROWS = 256
D = 1024
HD = 128
eps = 1e-06
SCALE = HD**-0.5
EVENT_AT = (0, 1, 2, 3, 4, 5, 12, 13, 6, 7, 8, 9, 10, 11, 14, 15)
ROW_AT = (4, 5, 0, 1, 2, 3, 12, 13, 6, 7, 8, 9, 10, 11, 14, 15)
NT = (((1,), (1,)), ((), ()))
BF = jnp.bfloat16
F32 = jnp.float32


def silu(z):
    h = z * 0.5
    return h + h * jnp.tanh(h)


def weight(s):
    h = (s * (0.5 * SCALE)).astype(BF)
    return h + h * jnp.tanh(h)


def layer_norm(x):
    mean = jnp.mean(x, axis=-1, keepdims=True)
    var = jnp.mean((x - mean) ** 2, axis=-1, keepdims=True)
    return (x - mean) / jnp.sqrt(var + eps)


def kernel(
    x_hbm,
    win_hbm,
    wout_hbm,
    hk_hbm,
    hv_hbm,
    hlen_hbm,
    cnt_hbm,
    pmap_hbm,
    out_ref,
    hlen_ref,
    cnt_ref,
    pmap_ref,
    x_v,
    n_v,
    win_v,
    hv_v,
    own_v,
    self_v,
    k_all,
    v_all,
    q_all,
    acc,
    osend,
    attn_v,
    wout_v,
    loc,
    k_snd,
    k_rcv,
    v_snd,
    v_rcv,
    q_snd,
    q_rcv,
    a_snd,
    a_rcv,
    w_snd,
    w_rcv,
):
    g = lax.axis_index("grp")
    s = lax.axis_index("seq")
    x, z, c = s // 8, (s // 2) % 4, s % 2
    xb, zb = x // 2, z // 2
    xh, zh = x + xb * (3 - 2 * x), z + zb * (3 - 2 * z)
    head = xh * 4 + zh * 2 + c

    def seq_of(x_, z_, c_):
        return x_ * 8 + z_ * 2 + c_

    def device(d, xb_, zb_):
        d2, d1, d0 = d // 4, (d // 2) % 2, d % 2
        xp = xh + d2 * (1 - 2 * xh)
        zp = zh + d1 * (1 - 2 * zh)
        cp = c + d0 * (1 - 2 * c)
        return (g, seq_of(xp + xb_ * (3 - 2 * xp), zp + zb_ * (3 - 2 * zp), cp)), xp * 4 + zp * 2 + cp

    def peer(d):
        return device(d, xb, zb)

    def across(d, core):
        return device(d, xb + (1 - core) * (1 - 2 * xb), zb + core * (1 - 2 * zb))

    row_partner = across(0, c)[0]
    event_partner = across(0, 1 - c)[0]

    def cols(h):
        return pl.ds(pl.multiple_of(h * HD, HD), HD)

    def block(i):
        return pl.ds(i * ROWS if isinstance(i, int) else pl.multiple_of(i * ROWS, ROWS), ROWS)

    def group(i):
        return pl.ds(i * 2 * ROWS if isinstance(i, int) else pl.multiple_of(i * 2 * ROWS, 2 * ROWS), 2 * ROWS)

    def ev(d):
        return block(EVENT_AT[d])

    def qs(d):
        return block(ROW_AT[d])

    def remote(src, dst, snd, rcv, dev):
        return pltpu.make_async_remote_copy(
            src_ref=src, dst_ref=dst, send_sem=snd, recv_sem=rcv, device_id=dev, device_id_type=MESH
        )

    barrier = pltpu.get_barrier_semaphore()
    senders = [peer(d)[0] for d in range(1, 8)] + [event_partner]
    for d in range(8):
        senders.append(across(d, (c + d % 2) % 2)[0])
    senders += [((g + d) % 4, s) for d in range(1, 4)]
    for dev in senders:
        pl.semaphore_signal(barrier, inc=1, device_id=dev, device_id_type=MESH)

    loads = [
        pltpu.make_async_copy(src, dst, loc.at[i])
        for i, (src, dst) in enumerate(
            [(x_hbm, x_v), (hlen_hbm, hlen_ref), (hv_hbm.at[0], hv_v)]
            + [(win_hbm.at[:, pl.ds(part * D, D)], win_v.at[part]) for part in (2, 3, 1, 0)]
            + [
                (wout_hbm, wout_v.at[block(g)]),
                (hk_hbm.at[0, :, cols(head)], k_all.at[ev(0)]),
                (cnt_hbm, cnt_ref),
                (pmap_hbm, pmap_ref),
            ]
        )
    ]
    for copy in loads:
        copy.start()

    def project(part, lo, n):
        ds = pl.ds(lo, n)
        own_v[part, :, ds] = silu(jnp.dot(n_v[...], win_v[part, :, ds], preferred_element_type=F32)).astype(BF)

    loads[0].wait()
    n_v[...] = layer_norm(x_v[...].astype(F32)).astype(BF)
    loads[1].wait()
    loads[2].wait()
    pos = s * ROWS + lax.broadcasted_iota(jnp.int32, (ROWS, D), 0)
    hv_v[...] = jnp.where(pos < hlen_ref[0], hv_v[...].astype(F32), 0.0).astype(BF)
    v_all[ev(0), :] = hv_v[:, cols(head)]
    loads[3].wait()
    project(2, 0, D)
    q_own = own_v.at[2]
    q_all[qs(0), :] = own_v[2, :, cols(head)]

    pl.semaphore_wait(barrier, len(senders))

    sends = []

    def go(copy):
        copy().start()
        sends.append(copy)

    def send_kv(d):
        dev, h = peer(d)
        go(lambda: remote(hk_hbm.at[0, :, cols(h)], k_all.at[ev(d)], k_snd.at[d], k_rcv.at[d], dev))
        go(lambda: remote(hv_v.at[:, cols(h)], v_all.at[ev(d)], v_snd.at[d], v_rcv.at[d], dev))

    def send_q(d):
        dev, h = peer(d)
        go(lambda: remote(q_own.at[:, cols(h)], q_all.at[qs(d)], q_snd.at[d], q_rcv.at[d], dev))

    def arrived(buf, rows, rcv, d):
        remote(buf.at[rows], buf.at[rows], rcv.at[d], rcv.at[d], event_partner).wait_recv()

    def await_kv(d):
        arrived(k_all, ev(d), k_rcv, d)
        arrived(v_all, ev(d), v_rcv, d)

    def await_q(d):
        arrived(q_all, qs(d), q_rcv, d)

    def pass_kv(d):
        if d:
            arrived(k_all, ev(d), k_rcv, d)
        k_src = k_all.at[ev(d)] if d else hk_hbm.at[0, :, cols(head)]
        go(lambda: remote(k_src, k_all.at[ev(8 + d)], k_snd.at[8 + d], k_rcv.at[8 + d], event_partner))
        if d:
            arrived(v_all, ev(d), v_rcv, d)
        go(lambda: remote(v_all.at[ev(d)], v_all.at[ev(8 + d)], v_snd.at[8 + d], v_rcv.at[8 + d], event_partner))

    def pass_q(d):
        if d:
            await_q(d)
        go(lambda: remote(q_all.at[qs(d)], q_all.at[qs(8 + d)], q_snd.at[8 + d], q_rcv.at[8 + d], row_partner))

    def w_rows(d, core):
        return pl.ds(pl.multiple_of(((g - d + 4) % 4) * 256 + core * 128, 128), 128)

    half = pl.ds(pl.multiple_of(c * 128, 128), 128)

    def send_w(d):
        dst = wout_v.at[w_rows(0, c)]
        go(lambda: remote(wout_hbm.at[half], dst, w_snd.at[d], w_rcv.at[d], ((g + d) % 4, s)))

    def pass_w(d):
        arrived(wout_v, w_rows(d, c), w_rcv, d)
        rows = wout_v.at[w_rows(d, c)]
        go(lambda: remote(rows, rows, w_snd.at[4 + d], w_rcv.at[4 + d], peer(1)[0]))

    send_kv(1)
    send_q(1)
    pass_kv(0)
    pass_q(0)
    for d in (2, 4, 3, 5):
        send_kv(d)
    for d in (2, 4, 3, 5):
        send_q(d)
    for d in (6, 7):
        send_kv(d)
    for d in (6, 7):
        send_q(d)
    for d in range(1, 4):
        send_w(d)

    for load in loads[4:7]:
        load.wait()
    pass_kv(1)
    pass_q(1)

    def rest(i, _):
        part = (2 - i) % 3 + (2 - i) // 2
        ds = pl.ds(0, D)
        own_v[part, :, ds] = silu(jnp.dot(n_v[...], win_v[part], preferred_element_type=F32)).astype(BF)
        return 0

    lax.fori_loop(0, 3, rest, 0)
    for h in range(HEADS):
        ds = pl.ds(h * HD, HD)
        dot = jnp.sum(own_v[2, :, ds].astype(F32) * own_v[3, :, ds].astype(F32), axis=-1, keepdims=True)
        self_v[:, ds] = silu(dot * SCALE).astype(BF).astype(F32) * own_v[1, :, ds].astype(F32)
    for d in (2, 4, 3, 5):
        pass_kv(d)

    def attend(rows, events):
        sc = lax.dot_general(q_all[rows, :], k_all[events, :], NT, preferred_element_type=F32)
        return jnp.dot(weight(sc), v_all[events, :], preferred_element_type=F32)

    loads[8].wait()

    def early(n, _):
        @pl.when(n == 1)
        def _():
            await_q(8)
            await_q(9)

        @pl.when(n == 2)
        def _():
            for d in (2, 4, 3, 5):
                pass_q(d)

        @pl.when(n == 4)
        def _():
            for d in range(8, 14):
                await_kv(d)

        @pl.when(n == 7)
        def _():
            pass_kv(6)

        @pl.when(n == 8)
        def _():
            for d in (10, 11, 12, 13):
                await_q(d)
            pass_kv(7)

        @pl.when(n == 10)
        def _():
            pass_q(6)
            pass_q(7)

        last = n // 8
        gr = (1 - last) * ((n + 2) % 4) + last * (n // 2)
        hf = (1 - last) * (n // 4) + last * (n % 2)
        events = pl.ds(pl.multiple_of(hf * 6 * ROWS, 6 * ROWS), 6 * ROWS)
        acc[hf, group(gr), :] = attend(group(gr), events)
        return 0

    lax.fori_loop(0, 12, early, 0)

    for d in range(1, 4):
        pass_w(d)

    def a_copy(d):
        if d < 8:
            dev = peer(d)[0]
        else:
            dev = across(d - 8, c)[0]
        return remote(osend.at[qs(d)], attn_v.at[d // 8, :, cols(head)], a_snd.at[d], a_rcv.at[d], dev)

    def send_sums(d):
        go(lambda: a_copy(d))

    for d in (14, 15):
        await_kv(d)
    late = pl.ds(12 * ROWS, 4 * ROWS)

    def finish(m, _):
        gr = (m + 3) % 6
        osend[group(gr), :] = (acc[0, group(gr), :] + acc[1, group(gr), :] + attend(group(gr), late)).astype(BF)
        for i, ds in enumerate(((8, 9), (10, 11), (12, 13), (2, 3), (4, 5), (1,))):

            @pl.when(m == i)
            def _():
                for d in ds:
                    send_sums(d)

        return 0

    lax.fori_loop(0, 6, finish, 0)
    attn_v[0, :, cols(head)] = osend[qs(0), :]

    def whole(m, _):
        @pl.when(m == 1)
        def _():
            await_q(14)
            await_q(15)

        osend[group(6 + m), :] = attend(group(6 + m), pl.ds(0, 16 * ROWS)).astype(BF)
        for i, ds in enumerate(((6, 7), (14, 15))):

            @pl.when(m == i)
            def _():
                for d in ds:
                    send_sums(d)

        return 0

    lax.fori_loop(0, 2, whole, 0)

    for d in range(1, 4):
        arrived(wout_v, w_rows(d, 1 - c), w_rcv, 4 + d)
    loads[7].wait()
    loads[9].wait()
    loads[10].wait()
    for d in range(1, 16):
        h = peer(d % 8)[1]
        remote(osend.at[qs(d)], attn_v.at[d // 8, :, cols(h)], a_snd.at[d], a_rcv.at[d], event_partner).wait_recv()

    attn = attn_v[0].astype(F32) + attn_v[1].astype(F32) + self_v[...]
    n_v[...] = (layer_norm(attn) * own_v[0].astype(F32)).astype(BF)

    def out_piece(p, _):
        ds = pl.ds(pl.multiple_of(p * 512, 512), 512)
        mixed = x_v[:, ds].astype(F32) + jnp.dot(n_v[...], wout_v[:, ds], preferred_element_type=F32)
        for i in range(ROWS // PANEL):
            number = pmap_ref[i] * PANEL + lax.broadcasted_iota(jnp.int32, (PANEL, 512), 0)
            keep = mixed[i * PANEL : (i + 1) * PANEL]
            out_ref[pl.ds(i * PANEL, PANEL), ds] = jnp.where(number < cnt_ref[0], keep, 0.0).astype(BF)
        return 0

    lax.fori_loop(0, 2, out_piece, 0)

    for copy in sends:
        copy().wait_send()


def per_device(cand_x, w_in, w_out, hist_keys, hist_values, hist_len, cand_count, panel_map):
    dma = pltpu.SemaphoreType.DMA
    return pl.pallas_call(
        kernel,
        out_shape=pltpu.VMEM((ROWS, D), BF),
        in_specs=[pl.BlockSpec(memory_space=pl.ANY)] * 8,
        out_specs=pl.BlockSpec(memory_space=pltpu.VMEM),
        scratch_shapes=[
            pltpu.SMEM((1,), jnp.int32),
            pltpu.SMEM((1,), jnp.int32),
            pltpu.SMEM((ROWS // PANEL,), jnp.int32),
            pltpu.VMEM((ROWS, D), BF),
            pltpu.VMEM((ROWS, D), BF),
            pltpu.VMEM((4, D, D), BF),
            pltpu.VMEM((ROWS, D), BF),
            pltpu.VMEM((4, ROWS, D), BF),
            pltpu.VMEM((ROWS, D), F32),
            pltpu.VMEM((16 * ROWS, HD), BF),
            pltpu.VMEM((16 * ROWS, HD), BF),
            pltpu.VMEM((16 * ROWS, HD), BF),
            pltpu.VMEM((2, 12 * ROWS, HD), F32),
            pltpu.VMEM((16 * ROWS, HD), BF),
            pltpu.VMEM((2, ROWS, D), BF),
            pltpu.VMEM((D, D), BF),
            dma((11,)),
            dma((16,)),
            dma((16,)),
            dma((16,)),
            dma((16,)),
            dma((16,)),
            dma((16,)),
            dma((16,)),
            dma((16,)),
            dma((8,)),
            dma((8,)),
        ],
        compiler_params=pltpu.CompilerParams(
            collective_id=0, has_side_effects=True, vmem_limit_bytes=48 * 2**20
        ),
    )(cand_x, w_in, w_out, hist_keys, hist_values, hist_len, cand_count, panel_map)


def solution(mesh):
    return jax.shard_map(
        per_device,
        mesh=mesh,
        in_specs=(
            P(("grp", "seq"), None),
            P(),
            P("grp", None),
            P("grp", "seq", None),
            P("grp", "seq", None),
            P("grp"),
            P("grp"),
            P(("grp", "seq")),
        ),
        out_specs=P(("grp", "seq"), None),
        check_vma=False,
    )
```

```python
import jax
import jax.numpy as jnp
from jax import lax
from jax.experimental import pallas as pl
from jax.experimental.pallas import tpu as pltpu
from jax.sharding import PartitionSpec as P

MESH = pl.DeviceIdType.MESH
HEADS = 8
PANEL = 32
ROWS = 256
D = 1024
HD = 128
eps = 1e-06
SCALE = HD**-0.5
EVENT_AT = (0, 1, 2, 3, 4, 5, 12, 13, 6, 7, 8, 9, 10, 11, 14, 15)
ROW_AT = (4, 5, 0, 1, 2, 3, 12, 13, 6, 7, 8, 9, 10, 11, 14, 15)
NT = (((1,), (1,)), ((), ()))
BF = jnp.bfloat16
F32 = jnp.float32


def silu(z):
    h = z * 0.5
    return h + h * jnp.tanh(h)


def weight(s):
    h = (s * (0.5 * SCALE)).astype(BF)
    return h + h * jnp.tanh(h)


def layer_norm(x):
    mean = jnp.mean(x, axis=-1, keepdims=True)
    var = jnp.mean((x - mean) ** 2, axis=-1, keepdims=True)
    return (x - mean) / jnp.sqrt(var + eps)


def kernel(
    x_hbm,
    win_hbm,
    wout_hbm,
    hk_hbm,
    hv_hbm,
    hlen_hbm,
    cnt_hbm,
    pmap_hbm,
    out_ref,
    hlen_ref,
    cnt_ref,
    pmap_ref,
    x_v,
    n_v,
    win_v,
    hv_v,
    own_v,
    self_v,
    k_all,
    v_all,
    q_all,
    acc,
    osend,
    attn_v,
    wout_v,
    loc,
    k_snd,
    k_rcv,
    v_snd,
    v_rcv,
    q_snd,
    q_rcv,
    a_snd,
    a_rcv,
    w_snd,
    w_rcv,
):
    g = lax.axis_index("grp")
    s = lax.axis_index("seq")
    x, z, c = s // 8, (s // 2) % 4, s % 2
    xb, zb = x // 2, z // 2
    xh, zh = x + xb * (3 - 2 * x), z + zb * (3 - 2 * z)
    head = xh * 4 + zh * 2 + c

    def seq_of(x_, z_, c_):
        return x_ * 8 + z_ * 2 + c_

    def device(d, xb_, zb_):
        d2, d1, d0 = d // 4, (d // 2) % 2, d % 2
        xp = xh + d2 * (1 - 2 * xh)
        zp = zh + d1 * (1 - 2 * zh)
        cp = c + d0 * (1 - 2 * c)
        return (g, seq_of(xp + xb_ * (3 - 2 * xp), zp + zb_ * (3 - 2 * zp), cp)), xp * 4 + zp * 2 + cp

    def peer(d):
        return device(d, xb, zb)

    def across(d, core):
        return device(d, xb + (1 - core) * (1 - 2 * xb), zb + core * (1 - 2 * zb))

    row_partner = across(0, c)[0]
    event_partner = across(0, 1 - c)[0]

    def cols(h):
        return pl.ds(pl.multiple_of(h * HD, HD), HD)

    def block(i):
        return pl.ds(i * ROWS if isinstance(i, int) else pl.multiple_of(i * ROWS, ROWS), ROWS)

    def group(i):
        return pl.ds(i * 2 * ROWS if isinstance(i, int) else pl.multiple_of(i * 2 * ROWS, 2 * ROWS), 2 * ROWS)

    def ev(d):
        return block(EVENT_AT[d])

    def qs(d):
        return block(ROW_AT[d])

    def remote(src, dst, snd, rcv, dev):
        return pltpu.make_async_remote_copy(
            src_ref=src, dst_ref=dst, send_sem=snd, recv_sem=rcv, device_id=dev, device_id_type=MESH
        )

    barrier = pltpu.get_barrier_semaphore()
    partners = [peer(d)[0] for d in range(1, 8)] + [row_partner, event_partner]
    partners += [((g + d) % 4, s) for d in range(1, 4)]
    for dev in partners:
        pl.semaphore_signal(barrier, inc=1, device_id=dev, device_id_type=MESH)

    loads = [
        pltpu.make_async_copy(src, dst, loc.at[i])
        for i, (src, dst) in enumerate(
            [(x_hbm, x_v), (hlen_hbm, hlen_ref), (hv_hbm.at[0], hv_v)]
            + [(win_hbm.at[:, pl.ds(part * D, D)], win_v.at[part]) for part in (2, 3, 1, 0)]
            + [
                (wout_hbm, wout_v.at[block(g)]),
                (hk_hbm.at[0, :, cols(head)], k_all.at[ev(0)]),
                (cnt_hbm, cnt_ref),
                (pmap_hbm, pmap_ref),
            ]
        )
    ]
    for i in (1, 2, 0, 3):
        loads[i].start()

    loads[1].wait()
    loads[2].wait()
    pos = s * ROWS + lax.broadcasted_iota(jnp.int32, (ROWS, D), 0)
    hv_v[...] = jnp.where(pos < hlen_ref[0], hv_v[...].astype(F32), 0.0).astype(BF)
    v_all[ev(0), :] = hv_v[:, cols(head)]
    loads[0].wait()
    n_v[...] = layer_norm(x_v[...].astype(F32)).astype(BF)
    for i in (4, 5, 6, 7, 8, 9, 10):
        loads[i].start()
    loads[3].wait()
    own_v[2] = silu(jnp.dot(n_v[...], win_v[2], preferred_element_type=F32)).astype(BF)
    q_all[qs(0), :] = own_v[2, :, cols(head)]

    pl.semaphore_wait(barrier, len(partners))

    sends = []

    def go(copy):
        copy().start()
        sends.append(copy)

    def send_k(d):
        dev, h = peer(d)
        go(lambda: remote(hk_hbm.at[0, :, cols(h)], k_all.at[ev(d)], k_snd.at[d], k_rcv.at[d], dev))

    def send_v(d):
        dev, h = peer(d)
        go(lambda: remote(hv_v.at[:, cols(h)], v_all.at[ev(d)], v_snd.at[d], v_rcv.at[d], dev))

    q_own = own_v.at[2]

    def send_q(d):
        dev, h = peer(d)
        go(lambda: remote(q_own.at[:, cols(h)], q_all.at[qs(d)], q_snd.at[d], q_rcv.at[d], dev))

    def arrived(buf, rows, rcv, d):
        remote(buf.at[rows], buf.at[rows], rcv.at[d], rcv.at[d], event_partner).wait_recv()

    def await_kv(d):
        arrived(k_all, ev(d), k_rcv, d)
        arrived(v_all, ev(d), v_rcv, d)

    def await_q(d):
        arrived(q_all, qs(d), q_rcv, d)

    def pass_k(d):
        if d:
            arrived(k_all, ev(d), k_rcv, d)
        k_src = k_all.at[ev(d)] if d else hk_hbm.at[0, :, cols(head)]
        go(lambda: remote(k_src, k_all.at[ev(8 + d)], k_snd.at[8 + d], k_rcv.at[8 + d], event_partner))

    def pass_v(d):
        if d:
            arrived(v_all, ev(d), v_rcv, d)
        go(lambda: remote(v_all.at[ev(d)], v_all.at[ev(8 + d)], v_snd.at[8 + d], v_rcv.at[8 + d], event_partner))

    def pass_kv(d):
        pass_k(d)
        pass_v(d)

    def pass_q(d):
        if d:
            await_q(d)
        go(lambda: remote(q_all.at[qs(d)], q_all.at[qs(8 + d)], q_snd.at[8 + d], q_rcv.at[8 + d], row_partner))

    def w_rows(d, core):
        return pl.ds(pl.multiple_of(((g - d + 4) % 4) * 256 + core * 128, 128), 128)

    half = pl.ds(pl.multiple_of(c * 128, 128), 128)

    def send_w(d):
        dst = wout_v.at[w_rows(0, c)]
        go(lambda: remote(wout_hbm.at[half], dst, w_snd.at[d], w_rcv.at[d], ((g + d) % 4, s)))

    def pass_w(d):
        arrived(wout_v, w_rows(d, c), w_rcv, d)
        rows = wout_v.at[w_rows(d, c)]
        go(lambda: remote(rows, rows, w_snd.at[4 + d], w_rcv.at[4 + d], peer(1)[0]))

    near = (2, 4, 3, 5)
    for d in near:
        send_k(d)
    send_k(1)
    pass_k(0)

    for d in near:
        send_v(d)
    send_v(1)
    pass_v(0)

    for d in near:
        send_q(d)
    send_q(1)
    pass_q(0)
    for d in (6, 7):
        send_k(d)
        send_v(d)
    for d in (6, 7):
        send_q(d)
    for d in range(1, 4):
        send_w(d)

    pass_kv(1)
    pass_q(1)
    for d in near:
        pass_k(d)
    for load in loads[4:7]:
        load.wait()

    def rest(i, _):
        part = (2 - i) % 3 + (2 - i) // 2
        ds = pl.ds(0, D)
        own_v[part, :, ds] = silu(jnp.dot(n_v[...], win_v[part], preferred_element_type=F32)).astype(BF)
        return 0

    lax.fori_loop(0, 3, rest, 0)
    for h in range(HEADS):
        ds = pl.ds(h * HD, HD)
        dot = jnp.sum(own_v[2, :, ds].astype(F32) * own_v[3, :, ds].astype(F32), axis=-1, keepdims=True)
        self_v[:, ds] = silu(dot * SCALE).astype(BF).astype(F32) * own_v[1, :, ds].astype(F32)
    for d in near:
        pass_v(d)

    def attend(rows, events):
        sc = lax.dot_general(q_all[rows, :], k_all[events, :], NT, preferred_element_type=F32)
        return jnp.dot(weight(sc), v_all[events, :], preferred_element_type=F32)

    loads[8].wait()

    def early(n, _):
        @pl.when(n == 1)
        def _():
            await_q(8)
            await_q(9)

        @pl.when(n == 2)
        def _():
            for d in near:
                pass_q(d)

        @pl.when(n == 4)
        def _():
            for d in range(8, 14):
                await_kv(d)

        @pl.when(n == 7)
        def _():
            for d in (10, 11, 12, 13):
                await_q(d)
            pass_kv(6)

        @pl.when(n == 8)
        def _():
            pass_kv(7)

        @pl.when(n == 9)
        def _():
            pass_q(6)
            pass_q(7)

        last = (n + 1) // 8
        gr = (1 - last) * ((n + 2 - 3 * (n // 4)) % 4) + last * ((n + 1) // 2)
        hf = (1 - last) * (n // 4) + last * ((n + 1) % 2)
        events = pl.ds(pl.multiple_of(hf * 6 * ROWS, 6 * ROWS), 6 * ROWS)
        acc[hf, group(gr), :] = attend(group(gr), events)
        return 0

    lax.fori_loop(0, 11, early, 0)

    for d in range(1, 4):
        pass_w(d)

    def a_copy(d):
        if d < 8:
            dev = peer(d)[0]
        else:
            dev = across(d - 8, c)[0]
        return remote(osend.at[qs(d)], attn_v.at[d // 8, :, cols(head)], a_snd.at[d], a_rcv.at[d], dev)

    def send_sums(d):
        go(lambda: a_copy(d))

    for d in (14, 15):
        await_kv(d)
    late = pl.ds(12 * ROWS, 4 * ROWS)

    def finish(m, _):
        gr = (m + 3) % 6
        osend[group(gr), :] = (acc[0, group(gr), :] + acc[1, group(gr), :] + attend(group(gr), late)).astype(BF)
        for i, ds in enumerate(((8, 9), (10, 11), (12, 13), (2, 3), (4, 5))):

            @pl.when(m == i)
            def _():
                for d in ds:
                    send_sums(d)

        return 0

    lax.fori_loop(0, 5, finish, 0)

    def whole(m, _):
        osend[group(7 - m), :] = attend(group(7 - m), pl.ds(0, 16 * ROWS)).astype(BF)
        for i, ds in enumerate(((14, 15), (6, 7))):

            @pl.when(m == i)
            def _():
                for d in ds:
                    send_sums(d)

        return 0

    await_q(14)
    await_q(15)
    lax.fori_loop(0, 2, whole, 0)

    osend[group(2), :] = (acc[0, group(2), :] + attend(group(2), pl.ds(6 * ROWS, 10 * ROWS))).astype(BF)
    send_sums(1)
    attn_v[0, :, cols(head)] = osend[qs(0), :]

    for d in range(1, 4):
        arrived(wout_v, w_rows(d, 1 - c), w_rcv, 4 + d)
    loads[7].wait()
    loads[9].wait()
    loads[10].wait()
    for d in range(1, 16):
        h = peer(d % 8)[1]
        remote(osend.at[qs(d)], attn_v.at[d // 8, :, cols(h)], a_snd.at[d], a_rcv.at[d], event_partner).wait_recv()

    attn = attn_v[0].astype(F32) + attn_v[1].astype(F32) + self_v[...]
    n_v[...] = (layer_norm(attn) * own_v[0].astype(F32)).astype(BF)

    def out_piece(p, _):
        ds = pl.ds(pl.multiple_of(p * 512, 512), 512)
        mixed = x_v[:, ds].astype(F32) + jnp.dot(n_v[...], wout_v[:, ds], preferred_element_type=F32)
        for i in range(ROWS // PANEL):
            number = pmap_ref[i] * PANEL + lax.broadcasted_iota(jnp.int32, (PANEL, 512), 0)
            keep = mixed[i * PANEL : (i + 1) * PANEL]
            out_ref[pl.ds(i * PANEL, PANEL), ds] = jnp.where(number < cnt_ref[0], keep, 0.0).astype(BF)
        return 0

    lax.fori_loop(0, 2, out_piece, 0)

    for copy in sends:
        copy().wait_send()


def per_device(cand_x, w_in, w_out, hist_keys, hist_values, hist_len, cand_count, panel_map):
    dma = pltpu.SemaphoreType.DMA
    return pl.pallas_call(
        kernel,
        out_shape=pltpu.VMEM((ROWS, D), BF),
        in_specs=[pl.BlockSpec(memory_space=pltpu.HBM)] * 8,
        out_specs=pl.BlockSpec(memory_space=pltpu.VMEM),
        scratch_shapes=[
            pltpu.SMEM((1,), jnp.int32),
            pltpu.SMEM((1,), jnp.int32),
            pltpu.SMEM((ROWS // PANEL,), jnp.int32),
            pltpu.VMEM((ROWS, D), BF),
            pltpu.VMEM((ROWS, D), BF),
            pltpu.VMEM((4, D, D), BF),
            pltpu.VMEM((ROWS, D), BF),
            pltpu.VMEM((4, ROWS, D), BF),
            pltpu.VMEM((ROWS, D), F32),
            pltpu.VMEM((16 * ROWS, HD), BF),
            pltpu.VMEM((16 * ROWS, HD), BF),
            pltpu.VMEM((16 * ROWS, HD), BF),
            pltpu.VMEM((2, 12 * ROWS, HD), F32),
            pltpu.VMEM((16 * ROWS, HD), BF),
            pltpu.VMEM((2, ROWS, D), BF),
            pltpu.VMEM((D, D), BF),
            dma((11,)),
            dma((16,)),
            dma((16,)),
            dma((16,)),
            dma((16,)),
            dma((16,)),
            dma((16,)),
            dma((16,)),
            dma((16,)),
            dma((8,)),
            dma((8,)),
        ],
        compiler_params=pltpu.CompilerParams(
            collective_id=0, has_side_effects=True, vmem_limit_bytes=56 * 2**20
        ),
    )(cand_x, w_in, w_out, hist_keys, hist_values, hist_len, cand_count, panel_map)


def solution(mesh):
    return jax.shard_map(
        per_device,
        mesh=mesh,
        in_specs=(
            P(("grp", "seq"), None),
            P(),
            P("grp", None),
            P("grp", "seq", None),
            P("grp", "seq", None),
            P("grp"),
            P("grp"),
            P(("grp", "seq")),
        ),
        out_specs=P(("grp", "seq"), None),
        check_vma=False,
    )
```

```python
import jax
import jax.numpy as jnp
from jax import lax
from jax.experimental import pallas as pl
from jax.experimental.pallas import tpu as pltpu
from jax.sharding import PartitionSpec as P

MESH = pl.DeviceIdType.MESH
HEADS = 8
PANEL = 32
ROWS = 256
D = 1024
HD = 128
eps = 1e-06
SCALE = HD**-0.5
EVENT_AT = (0, 1, 2, 3, 4, 5, 12, 13, 6, 7, 8, 9, 10, 11, 14, 15)
ROW_AT = (4, 5, 0, 1, 2, 3, 12, 13, 6, 7, 8, 9, 10, 11, 14, 15)
NT = (((1,), (1,)), ((), ()))
BF = jnp.bfloat16
F32 = jnp.float32


def silu(z):
    h = z * 0.5
    return h + h * jnp.tanh(h)


def weight(s):
    h = (s * (0.5 * SCALE)).astype(BF)
    return h + h * jnp.tanh(h)


def layer_norm(x):
    mean = jnp.mean(x, axis=-1, keepdims=True)
    var = jnp.mean((x - mean) ** 2, axis=-1, keepdims=True)
    return (x - mean) / jnp.sqrt(var + eps)


def kernel(
    x_hbm,
    win_hbm,
    wout_hbm,
    hk_hbm,
    hv_hbm,
    hlen_hbm,
    cnt_hbm,
    pmap_hbm,
    out_ref,
    hlen_ref,
    cnt_ref,
    pmap_ref,
    x_v,
    n_v,
    win_v,
    hv_v,
    own_v,
    self_v,
    k_all,
    v_all,
    q_all,
    acc,
    osend,
    attn_v,
    wout_v,
    loc,
    k_snd,
    k_rcv,
    v_snd,
    v_rcv,
    q_snd,
    q_rcv,
    a_snd,
    a_rcv,
    w_snd,
    w_rcv,
):
    g = lax.axis_index("grp")
    s = lax.axis_index("seq")
    x, z, c = s // 8, (s // 2) % 4, s % 2
    xb, zb = x // 2, z // 2
    xh, zh = x + xb * (3 - 2 * x), z + zb * (3 - 2 * z)
    head = xh * 4 + zh * 2 + c

    def seq_of(x_, z_, c_):
        return x_ * 8 + z_ * 2 + c_

    def device(d, xb_, zb_):
        d2, d1, d0 = d // 4, (d // 2) % 2, d % 2
        xp = xh + d2 * (1 - 2 * xh)
        zp = zh + d1 * (1 - 2 * zh)
        cp = c + d0 * (1 - 2 * c)
        return (g, seq_of(xp + xb_ * (3 - 2 * xp), zp + zb_ * (3 - 2 * zp), cp)), xp * 4 + zp * 2 + cp

    def peer(d):
        return device(d, xb, zb)

    def across(d, core):
        return device(d, xb + (1 - core) * (1 - 2 * xb), zb + core * (1 - 2 * zb))

    row_partner = across(0, c)[0]
    event_partner = across(0, 1 - c)[0]

    def cols(h):
        return pl.ds(pl.multiple_of(h * HD, HD), HD)

    def block(i):
        return pl.ds(i * ROWS if isinstance(i, int) else pl.multiple_of(i * ROWS, ROWS), ROWS)

    def group(i):
        return pl.ds(i * 2 * ROWS if isinstance(i, int) else pl.multiple_of(i * 2 * ROWS, 2 * ROWS), 2 * ROWS)

    def ev(d):
        return block(EVENT_AT[d])

    def qs(d):
        return block(ROW_AT[d])

    def remote(src, dst, snd, rcv, dev):
        return pltpu.make_async_remote_copy(
            src_ref=src, dst_ref=dst, send_sem=snd, recv_sem=rcv, device_id=dev, device_id_type=MESH
        )

    barrier = pltpu.get_barrier_semaphore()
    partners = [peer(d)[0] for d in range(1, 8)] + [row_partner, event_partner]
    partners += [((g + d) % 4, s) for d in range(1, 4)]
    for dev in partners:
        pl.semaphore_signal(barrier, inc=1, device_id=dev, device_id_type=MESH)

    loads = [
        pltpu.make_async_copy(src, dst, loc.at[i])
        for i, (src, dst) in enumerate(
            [(x_hbm, x_v), (hlen_hbm, hlen_ref), (hv_hbm.at[0], hv_v)]
            + [(win_hbm.at[:, pl.ds(part * D, D)], win_v.at[part]) for part in (2, 3, 1, 0)]
            + [
                (wout_hbm, wout_v.at[block(g)]),
                (hk_hbm.at[0, :, cols(head)], k_all.at[ev(0)]),
                (cnt_hbm, cnt_ref),
                (pmap_hbm, pmap_ref),
            ]
        )
    ]
    for i in (1, 2, 0, 3):
        loads[i].start()

    loads[1].wait()
    loads[2].wait()
    pos = s * ROWS + lax.broadcasted_iota(jnp.int32, (ROWS, D), 0)
    hv_v[...] = jnp.where(pos < hlen_ref[0], hv_v[...].astype(F32), 0.0).astype(BF)
    v_all[ev(0), :] = hv_v[:, cols(head)]
    loads[0].wait()
    n_v[...] = layer_norm(x_v[...].astype(F32)).astype(BF)
    pl.semaphore_wait(barrier, len(partners))

    sends = []

    def go(copy):
        copy().start()
        sends.append(copy)

    def send_k(d):
        dev, h = peer(d)
        go(lambda: remote(hk_hbm.at[0, :, cols(h)], k_all.at[ev(d)], k_snd.at[d], k_rcv.at[d], dev))

    def send_v(d):
        dev, h = peer(d)
        go(lambda: remote(hv_v.at[:, cols(h)], v_all.at[ev(d)], v_snd.at[d], v_rcv.at[d], dev))

    q_own = own_v.at[2]

    def send_q(d):
        dev, h = peer(d)
        go(lambda: remote(q_own.at[:, cols(h)], q_all.at[qs(d)], q_snd.at[d], q_rcv.at[d], dev))

    def arrived(buf, rows, rcv, d):
        remote(buf.at[rows], buf.at[rows], rcv.at[d], rcv.at[d], event_partner).wait_recv()

    def await_kv(d):
        arrived(k_all, ev(d), k_rcv, d)
        arrived(v_all, ev(d), v_rcv, d)

    def await_q(d):
        arrived(q_all, qs(d), q_rcv, d)

    def pass_k(d):
        if d:
            arrived(k_all, ev(d), k_rcv, d)
        k_src = k_all.at[ev(d)] if d else hk_hbm.at[0, :, cols(head)]
        go(lambda: remote(k_src, k_all.at[ev(8 + d)], k_snd.at[8 + d], k_rcv.at[8 + d], event_partner))

    def pass_v(d):
        if d:
            arrived(v_all, ev(d), v_rcv, d)
        go(lambda: remote(v_all.at[ev(d)], v_all.at[ev(8 + d)], v_snd.at[8 + d], v_rcv.at[8 + d], event_partner))

    def pass_kv(d):
        pass_k(d)
        pass_v(d)

    def pass_q(d):
        if d:
            await_q(d)
        go(lambda: remote(q_all.at[qs(d)], q_all.at[qs(8 + d)], q_snd.at[8 + d], q_rcv.at[8 + d], row_partner))

    def w_rows(d, core):
        return pl.ds(pl.multiple_of(((g - d + 4) % 4) * 256 + core * 128, 128), 128)

    half = pl.ds(pl.multiple_of(c * 128, 128), 128)

    def send_w(d):
        dst = wout_v.at[w_rows(0, c)]
        go(lambda: remote(wout_hbm.at[half], dst, w_snd.at[d], w_rcv.at[d], ((g + d) % 4, s)))

    def pass_w(d):
        arrived(wout_v, w_rows(d, c), w_rcv, d)
        rows = wout_v.at[w_rows(d, c)]
        go(lambda: remote(rows, rows, w_snd.at[4 + d], w_rcv.at[4 + d], peer(1)[0]))

    near = (2, 4, 3, 5)
    for d in near:
        send_k(d)
    send_k(1)
    pass_k(0)

    for d in near:
        send_v(d)
    send_v(1)
    pass_v(0)

    for i in (4, 5, 6, 7, 8, 9, 10):
        loads[i].start()
    loads[3].wait()
    own_v[2] = silu(jnp.dot(n_v[...], win_v[2], preferred_element_type=F32)).astype(BF)
    q_all[qs(0), :] = own_v[2, :, cols(head)]
    for d in near:
        send_q(d)
    send_q(1)
    pass_q(0)
    for d in (6, 7):
        send_k(d)
        send_v(d)
    for d in (6, 7):
        send_q(d)
    for d in range(1, 4):
        send_w(d)

    pass_kv(1)
    pass_q(1)
    for d in near:
        pass_k(d)
    for load in loads[4:7]:
        load.wait()

    def rest(i, _):
        part = (2 - i) % 3 + (2 - i) // 2
        ds = pl.ds(0, D)
        own_v[part, :, ds] = silu(jnp.dot(n_v[...], win_v[part], preferred_element_type=F32)).astype(BF)
        return 0

    lax.fori_loop(0, 3, rest, 0)
    for h in range(HEADS):
        ds = pl.ds(h * HD, HD)
        dot = jnp.sum(own_v[2, :, ds].astype(F32) * own_v[3, :, ds].astype(F32), axis=-1, keepdims=True)
        self_v[:, ds] = silu(dot * SCALE).astype(BF).astype(F32) * own_v[1, :, ds].astype(F32)
    for d in near:
        pass_v(d)

    def attend(rows, events):
        sc = lax.dot_general(q_all[rows, :], k_all[events, :], NT, preferred_element_type=F32)
        return jnp.dot(weight(sc), v_all[events, :], preferred_element_type=F32)

    loads[8].wait()

    def early(n, _):
        @pl.when(n == 1)
        def _():
            await_q(8)
            await_q(9)

        @pl.when(n == 2)
        def _():
            for d in near:
                pass_q(d)

        @pl.when(n == 4)
        def _():
            for d in range(8, 14):
                await_kv(d)

        @pl.when(n == 5)
        def _():
            pass_kv(6)
            pass_kv(7)

        @pl.when(n == 6)
        def _():
            await_q(10)
            await_q(11)

        @pl.when(n == 7)
        def _():
            pass_q(6)
            pass_q(7)
            await_q(12)
            await_q(13)

        last = n // 6
        gr = (1 - last) * ((n + 2 - 2 * (n // 4)) % 4) + last * (1 + n // 2)
        hf = (1 - last) * (n // 4) + last * (n % 2)
        events = pl.ds(pl.multiple_of(hf * 6 * ROWS, 6 * ROWS), 6 * ROWS)
        acc[hf, group(gr), :] = attend(group(gr), events)
        return 0

    lax.fori_loop(0, 10, early, 0)

    for d in range(1, 4):
        pass_w(d)

    def a_copy(d):
        if d < 8:
            dev = peer(d)[0]
        else:
            dev = across(d - 8, c)[0]
        return remote(osend.at[qs(d)], attn_v.at[d // 8, :, cols(head)], a_snd.at[d], a_rcv.at[d], dev)

    def send_sums(d):
        go(lambda: a_copy(d))

    for d in (14, 15):
        await_kv(d)
    late = pl.ds(12 * ROWS, 4 * ROWS)

    def finish(m, _):
        gr = (m + 4) % 6
        osend[group(gr), :] = (acc[0, group(gr), :] + acc[1, group(gr), :] + attend(group(gr), late)).astype(BF)
        for i, ds in enumerate(((10, 11), (12, 13), (2, 3), (4, 5))):

            @pl.when(m == i)
            def _():
                for d in ds:
                    send_sums(d)

        return 0

    lax.fori_loop(0, 4, finish, 0)

    def whole(m, _):
        osend[group(7 - m), :] = attend(group(7 - m), pl.ds(0, 16 * ROWS)).astype(BF)
        for i, ds in enumerate(((14, 15), (6, 7))):

            @pl.when(m == i)
            def _():
                for d in ds:
                    send_sums(d)

        return 0

    await_q(14)
    await_q(15)
    lax.fori_loop(0, 2, whole, 0)

    def near_rows(m, _):
        gr = 3 - m
        osend[group(gr), :] = (acc[0, group(gr), :] + attend(group(gr), pl.ds(6 * ROWS, 10 * ROWS))).astype(BF)
        for i, ds in enumerate(((8, 9), (1,))):

            @pl.when(m == i)
            def _():
                for d in ds:
                    send_sums(d)

        return 0

    lax.fori_loop(0, 2, near_rows, 0)
    attn_v[0, :, cols(head)] = osend[qs(0), :]

    for d in range(1, 4):
        arrived(wout_v, w_rows(d, 1 - c), w_rcv, 4 + d)
    loads[7].wait()
    loads[9].wait()
    loads[10].wait()
    for d in range(1, 16):
        h = peer(d % 8)[1]
        remote(osend.at[qs(d)], attn_v.at[d // 8, :, cols(h)], a_snd.at[d], a_rcv.at[d], event_partner).wait_recv()

    attn = attn_v[0].astype(F32) + attn_v[1].astype(F32) + self_v[...]
    n_v[...] = (layer_norm(attn) * own_v[0].astype(F32)).astype(BF)

    def out_piece(p, _):
        ds = pl.ds(pl.multiple_of(p * 512, 512), 512)
        mixed = x_v[:, ds].astype(F32) + jnp.dot(n_v[...], wout_v[:, ds], preferred_element_type=F32)
        for i in range(ROWS // PANEL):
            number = pmap_ref[i] * PANEL + lax.broadcasted_iota(jnp.int32, (PANEL, 512), 0)
            keep = mixed[i * PANEL : (i + 1) * PANEL]
            out_ref[pl.ds(i * PANEL, PANEL), ds] = jnp.where(number < cnt_ref[0], keep, 0.0).astype(BF)
        return 0

    lax.fori_loop(0, 2, out_piece, 0)

    for copy in sends:
        copy().wait_send()


def per_device(cand_x, w_in, w_out, hist_keys, hist_values, hist_len, cand_count, panel_map):
    dma = pltpu.SemaphoreType.DMA
    return pl.pallas_call(
        kernel,
        out_shape=pltpu.VMEM((ROWS, D), BF),
        in_specs=[pl.BlockSpec(memory_space=pltpu.HBM)] * 8,
        out_specs=pl.BlockSpec(memory_space=pltpu.VMEM),
        scratch_shapes=[
            pltpu.SMEM((1,), jnp.int32),
            pltpu.SMEM((1,), jnp.int32),
            pltpu.SMEM((ROWS // PANEL,), jnp.int32),
            pltpu.VMEM((ROWS, D), BF),
            pltpu.VMEM((ROWS, D), BF),
            pltpu.VMEM((4, D, D), BF),
            pltpu.VMEM((ROWS, D), BF),
            pltpu.VMEM((4, ROWS, D), BF),
            pltpu.VMEM((ROWS, D), F32),
            pltpu.VMEM((16 * ROWS, HD), BF),
            pltpu.VMEM((16 * ROWS, HD), BF),
            pltpu.VMEM((16 * ROWS, HD), BF),
            pltpu.VMEM((2, 12 * ROWS, HD), F32),
            pltpu.VMEM((16 * ROWS, HD), BF),
            pltpu.VMEM((2, ROWS, D), BF),
            pltpu.VMEM((D, D), BF),
            dma((11,)),
            dma((16,)),
            dma((16,)),
            dma((16,)),
            dma((16,)),
            dma((16,)),
            dma((16,)),
            dma((16,)),
            dma((16,)),
            dma((8,)),
            dma((8,)),
        ],
        compiler_params=pltpu.CompilerParams(
            collective_id=0, has_side_effects=True, vmem_limit_bytes=56 * 2**20
        ),
    )(cand_x, w_in, w_out, hist_keys, hist_values, hist_len, cand_count, panel_map)


def solution(mesh):
    return jax.shard_map(
        per_device,
        mesh=mesh,
        in_specs=(
            P(("grp", "seq"), None),
            P(),
            P("grp", None),
            P("grp", "seq", None),
            P("grp", "seq", None),
            P("grp"),
            P("grp"),
            P(("grp", "seq")),
        ),
        out_specs=P(("grp", "seq"), None),
        check_vma=False,
    )
```

```python
import jax
import jax.numpy as jnp
from jax import lax
from jax.experimental import pallas as pl
from jax.experimental.pallas import tpu as pltpu
from jax.sharding import PartitionSpec as P

MESH = pl.DeviceIdType.MESH
HEADS = 8
PANEL = 32
ROWS = 256
D = 1024
HD = 128
eps = 1e-06
SCALE = HD**-0.5
EVENT_AT = (0, 1, 2, 3, 4, 5, 12, 13, 6, 7, 8, 9, 10, 11, 14, 15)
ROW_AT = (4, 5, 0, 1, 2, 3, 12, 13, 6, 7, 8, 9, 10, 11, 14, 15)
NT = (((1,), (1,)), ((), ()))
BF = jnp.bfloat16
F32 = jnp.float32


def silu(z):
    h = z * 0.5
    return h + h * jnp.tanh(h)


def weight(s):
    h = (s * (0.5 * SCALE)).astype(BF)
    return h + h * jnp.tanh(h)


def layer_norm(x):
    mean = jnp.mean(x, axis=-1, keepdims=True)
    var = jnp.mean((x - mean) ** 2, axis=-1, keepdims=True)
    return (x - mean) / jnp.sqrt(var + eps)


def kernel(
    x_hbm,
    win_hbm,
    wout_hbm,
    hk_hbm,
    hv_hbm,
    hlen_hbm,
    cnt_hbm,
    pmap_hbm,
    out_ref,
    hlen_ref,
    cnt_ref,
    pmap_ref,
    x_v,
    n_v,
    win_v,
    hv_v,
    own_v,
    self_v,
    k_all,
    v_all,
    q_all,
    acc,
    osend,
    attn_v,
    wout_v,
    loc,
    k_snd,
    k_rcv,
    v_snd,
    v_rcv,
    q_snd,
    q_rcv,
    a_snd,
    a_rcv,
    w_snd,
    w_rcv,
):
    g = lax.axis_index("grp")
    s = lax.axis_index("seq")
    x, z, c = s // 8, (s // 2) % 4, s % 2
    xb, zb = x // 2, z // 2
    xh, zh = x + xb * (3 - 2 * x), z + zb * (3 - 2 * z)
    head = xh * 4 + zh * 2 + c

    def seq_of(x_, z_, c_):
        return x_ * 8 + z_ * 2 + c_

    def device(d, xb_, zb_):
        d2, d1, d0 = d // 4, (d // 2) % 2, d % 2
        xp = xh + d2 * (1 - 2 * xh)
        zp = zh + d1 * (1 - 2 * zh)
        cp = c + d0 * (1 - 2 * c)
        return (g, seq_of(xp + xb_ * (3 - 2 * xp), zp + zb_ * (3 - 2 * zp), cp)), xp * 4 + zp * 2 + cp

    def peer(d):
        return device(d, xb, zb)

    def across(d, core):
        return device(d, xb + (1 - core) * (1 - 2 * xb), zb + core * (1 - 2 * zb))

    row_partner = across(0, c)[0]
    event_partner = across(0, 1 - c)[0]

    def cols(h):
        return pl.ds(pl.multiple_of(h * HD, HD), HD)

    def block(i):
        return pl.ds(i * ROWS if isinstance(i, int) else pl.multiple_of(i * ROWS, ROWS), ROWS)

    def group(i):
        return pl.ds(i * 2 * ROWS if isinstance(i, int) else pl.multiple_of(i * 2 * ROWS, 2 * ROWS), 2 * ROWS)

    def ev(d):
        return block(EVENT_AT[d])

    def qs(d):
        return block(ROW_AT[d])

    def remote(src, dst, snd, rcv, dev):
        return pltpu.make_async_remote_copy(
            src_ref=src, dst_ref=dst, send_sem=snd, recv_sem=rcv, device_id=dev, device_id_type=MESH
        )

    barrier = pltpu.get_barrier_semaphore()
    partners = [peer(d)[0] for d in range(1, 8)] + [row_partner, event_partner]
    partners += [((g + d) % 4, s) for d in range(1, 4)]
    for dev in partners:
        pl.semaphore_signal(barrier, inc=1, device_id=dev, device_id_type=MESH)

    loads = [
        pltpu.make_async_copy(src, dst, loc.at[i])
        for i, (src, dst) in enumerate(
            [(x_hbm, x_v), (hlen_hbm, hlen_ref), (hv_hbm.at[0], hv_v)]
            + [(win_hbm.at[:, pl.ds(part * D, D)], win_v.at[part]) for part in (2, 3, 1, 0)]
            + [
                (wout_hbm, wout_v.at[block(g)]),
                (hk_hbm.at[0, :, cols(head)], k_all.at[ev(0)]),
                (cnt_hbm, cnt_ref),
                (pmap_hbm, pmap_ref),
            ]
        )
    ]
    for i in (1, 2, 0, 3):
        loads[i].start()

    loads[1].wait()
    loads[2].wait()
    pos = s * ROWS + lax.broadcasted_iota(jnp.int32, (ROWS, D), 0)
    hv_v[...] = jnp.where(pos < hlen_ref[0], hv_v[...].astype(F32), 0.0).astype(BF)
    v_all[ev(0), :] = hv_v[:, cols(head)]
    loads[0].wait()
    n_v[...] = layer_norm(x_v[...].astype(F32)).astype(BF)
    pl.semaphore_wait(barrier, len(partners))

    sends = []

    def go(copy):
        copy().start()
        sends.append(copy)

    def send_k(d):
        dev, h = peer(d)
        go(lambda: remote(hk_hbm.at[0, :, cols(h)], k_all.at[ev(d)], k_snd.at[d], k_rcv.at[d], dev))

    def send_v(d):
        dev, h = peer(d)
        go(lambda: remote(hv_v.at[:, cols(h)], v_all.at[ev(d)], v_snd.at[d], v_rcv.at[d], dev))

    q_own = own_v.at[2]

    def send_q(d):
        dev, h = peer(d)
        go(lambda: remote(q_own.at[:, cols(h)], q_all.at[qs(d)], q_snd.at[d], q_rcv.at[d], dev))

    def arrived(buf, rows, rcv, d):
        remote(buf.at[rows], buf.at[rows], rcv.at[d], rcv.at[d], event_partner).wait_recv()

    def await_kv(d):
        arrived(k_all, ev(d), k_rcv, d)
        arrived(v_all, ev(d), v_rcv, d)

    def await_q(d):
        arrived(q_all, qs(d), q_rcv, d)

    def pass_k(d):
        if d:
            arrived(k_all, ev(d), k_rcv, d)
        k_src = k_all.at[ev(d)] if d else hk_hbm.at[0, :, cols(head)]
        go(lambda: remote(k_src, k_all.at[ev(8 + d)], k_snd.at[8 + d], k_rcv.at[8 + d], event_partner))

    def pass_v(d):
        if d:
            arrived(v_all, ev(d), v_rcv, d)
        go(lambda: remote(v_all.at[ev(d)], v_all.at[ev(8 + d)], v_snd.at[8 + d], v_rcv.at[8 + d], event_partner))

    def pass_kv(d):
        pass_k(d)
        pass_v(d)

    def pass_q(d):
        if d:
            await_q(d)
        go(lambda: remote(q_all.at[qs(d)], q_all.at[qs(8 + d)], q_snd.at[8 + d], q_rcv.at[8 + d], row_partner))

    def w_rows(d, core):
        return pl.ds(pl.multiple_of(((g - d + 4) % 4) * 256 + core * 128, 128), 128)

    half = pl.ds(pl.multiple_of(c * 128, 128), 128)

    def send_w(d):
        dst = wout_v.at[w_rows(0, c)]
        go(lambda: remote(wout_hbm.at[half], dst, w_snd.at[d], w_rcv.at[d], ((g + d) % 4, s)))

    def pass_w(d):
        arrived(wout_v, w_rows(d, c), w_rcv, d)
        rows = wout_v.at[w_rows(d, c)]
        go(lambda: remote(rows, rows, w_snd.at[4 + d], w_rcv.at[4 + d], peer(1)[0]))

    near = (2, 4, 3, 5)
    for d in near:
        send_k(d)
    send_k(1)
    pass_k(0)

    for d in near:
        send_v(d)
    send_v(1)
    pass_v(0)

    for i in (4, 5, 6, 7, 8, 9, 10):
        loads[i].start()
    loads[3].wait()
    own_v[2] = silu(jnp.dot(n_v[...], win_v[2], preferred_element_type=F32)).astype(BF)
    q_all[qs(0), :] = own_v[2, :, cols(head)]
    for d in near:
        send_q(d)
    send_q(1)
    pass_q(0)
    for d in (6, 7):
        send_k(d)
        send_v(d)
    for d in (6, 7):
        send_q(d)
    for d in range(1, 4):
        send_w(d)

    pass_kv(1)
    pass_q(1)
    for load in loads[4:7]:
        load.wait()

    def rest(i, _):
        part = (2 - i) % 3 + (2 - i) // 2
        ds = pl.ds(0, D)
        own_v[part, :, ds] = silu(jnp.dot(n_v[...], win_v[part], preferred_element_type=F32)).astype(BF)
        return 0

    lax.fori_loop(0, 2, rest, 0)
    for d in near:
        pass_k(d)
    lax.fori_loop(2, 3, rest, 0)
    for h in range(HEADS):
        ds = pl.ds(h * HD, HD)
        dot = jnp.sum(own_v[2, :, ds].astype(F32) * own_v[3, :, ds].astype(F32), axis=-1, keepdims=True)
        self_v[:, ds] = silu(dot * SCALE).astype(BF).astype(F32) * own_v[1, :, ds].astype(F32)
    for d in near:
        pass_v(d)

    def attend(rows, events):
        sc = lax.dot_general(q_all[rows, :], k_all[events, :], NT, preferred_element_type=F32)
        return jnp.dot(weight(sc), v_all[events, :], preferred_element_type=F32)

    loads[8].wait()

    def early(n, _):
        @pl.when(n == 1)
        def _():
            await_q(8)
            await_q(9)

        @pl.when(n == 2)
        def _():
            for d in near:
                pass_q(d)

        @pl.when(n == 4)
        def _():
            for d in range(8, 14):
                await_kv(d)

        @pl.when(n == 5)
        def _():
            pass_kv(6)
            pass_kv(7)

        gr = (n + 2 - 2 * (n // 4)) % 4
        hf = n // 4
        events = pl.ds(pl.multiple_of(hf * 6 * ROWS, 6 * ROWS), 6 * ROWS)
        acc[hf, group(gr), :] = attend(group(gr), events)
        return 0

    lax.fori_loop(0, 6, early, 0)

    def partner_rows(m, _):
        @pl.when(m == 0)
        def _():
            await_q(10)
            await_q(11)

        @pl.when(m == 1)
        def _():
            pass_q(6)
            pass_q(7)
            await_q(12)
            await_q(13)

        acc[0, group(4 + m), :] = attend(group(4 + m), pl.ds(0, 12 * ROWS))
        acc[1, group(4 + m), :] = jnp.zeros((2 * ROWS, HD), F32)
        return 0

    lax.fori_loop(0, 2, partner_rows, 0)

    for d in range(1, 4):
        pass_w(d)

    def a_copy(d):
        if d < 8:
            dev = peer(d)[0]
        else:
            dev = across(d - 8, c)[0]
        return remote(osend.at[qs(d)], attn_v.at[d // 8, :, cols(head)], a_snd.at[d], a_rcv.at[d], dev)

    def send_sums(d):
        go(lambda: a_copy(d))

    for d in (14, 15):
        await_kv(d)
    late = pl.ds(12 * ROWS, 4 * ROWS)

    def finish(m, _):
        gr = (m + 4) % 6
        osend[group(gr), :] = (acc[0, group(gr), :] + acc[1, group(gr), :] + attend(group(gr), late)).astype(BF)
        for i, ds in enumerate(((10, 11), (12, 13), (2, 3), (4, 5))):

            @pl.when(m == i)
            def _():
                for d in ds:
                    send_sums(d)

        return 0

    lax.fori_loop(0, 4, finish, 0)

    def whole(m, _):
        osend[group(7 - m), :] = attend(group(7 - m), pl.ds(0, 16 * ROWS)).astype(BF)
        for i, ds in enumerate(((14, 15), (6, 7))):

            @pl.when(m == i)
            def _():
                for d in ds:
                    send_sums(d)

        return 0

    await_q(14)
    await_q(15)
    lax.fori_loop(0, 2, whole, 0)

    def near_rows(m, _):
        gr = 3 - m
        osend[group(gr), :] = (acc[0, group(gr), :] + attend(group(gr), pl.ds(6 * ROWS, 10 * ROWS))).astype(BF)
        for i, ds in enumerate(((8, 9), (1,))):

            @pl.when(m == i)
            def _():
                for d in ds:
                    send_sums(d)

        return 0

    lax.fori_loop(0, 2, near_rows, 0)
    attn_v[0, :, cols(head)] = osend[qs(0), :]

    for d in range(1, 4):
        arrived(wout_v, w_rows(d, 1 - c), w_rcv, 4 + d)
    loads[7].wait()
    loads[9].wait()
    loads[10].wait()
    for d in range(1, 16):
        h = peer(d % 8)[1]
        remote(osend.at[qs(d)], attn_v.at[d // 8, :, cols(h)], a_snd.at[d], a_rcv.at[d], event_partner).wait_recv()

    attn = attn_v[0].astype(F32) + attn_v[1].astype(F32) + self_v[...]
    n_v[...] = (layer_norm(attn) * own_v[0].astype(F32)).astype(BF)

    mixed = x_v[...].astype(F32) + jnp.dot(n_v[...], wout_v[...], preferred_element_type=F32)
    for i in range(ROWS // PANEL):
        number = pmap_ref[i] * PANEL + lax.broadcasted_iota(jnp.int32, (PANEL, D), 0)
        keep = mixed[i * PANEL : (i + 1) * PANEL]
        out_ref[pl.ds(i * PANEL, PANEL), :] = jnp.where(number < cnt_ref[0], keep, 0.0).astype(BF)

    for copy in sends:
        copy().wait_send()


def per_device(cand_x, w_in, w_out, hist_keys, hist_values, hist_len, cand_count, panel_map):
    dma = pltpu.SemaphoreType.DMA
    return pl.pallas_call(
        kernel,
        out_shape=pltpu.VMEM((ROWS, D), BF),
        in_specs=[pl.BlockSpec(memory_space=pltpu.HBM)] * 8,
        out_specs=pl.BlockSpec(memory_space=pltpu.VMEM),
        scratch_shapes=[
            pltpu.SMEM((1,), jnp.int32),
            pltpu.SMEM((1,), jnp.int32),
            pltpu.SMEM((ROWS // PANEL,), jnp.int32),
            pltpu.VMEM((ROWS, D), BF),
            pltpu.VMEM((ROWS, D), BF),
            pltpu.VMEM((4, D, D), BF),
            pltpu.VMEM((ROWS, D), BF),
            pltpu.VMEM((4, ROWS, D), BF),
            pltpu.VMEM((ROWS, D), F32),
            pltpu.VMEM((16 * ROWS, HD), BF),
            pltpu.VMEM((16 * ROWS, HD), BF),
            pltpu.VMEM((16 * ROWS, HD), BF),
            pltpu.VMEM((2, 12 * ROWS, HD), F32),
            pltpu.VMEM((16 * ROWS, HD), BF),
            pltpu.VMEM((2, ROWS, D), BF),
            pltpu.VMEM((D, D), BF),
            dma((11,)),
            dma((16,)),
            dma((16,)),
            dma((16,)),
            dma((16,)),
            dma((16,)),
            dma((16,)),
            dma((16,)),
            dma((16,)),
            dma((8,)),
            dma((8,)),
        ],
        compiler_params=pltpu.CompilerParams(
            collective_id=0, has_side_effects=True, vmem_limit_bytes=56 * 2**20
        ),
    )(cand_x, w_in, w_out, hist_keys, hist_values, hist_len, cand_count, panel_map)


def solution(mesh):
    return jax.shard_map(
        per_device,
        mesh=mesh,
        in_specs=(
            P(("grp", "seq"), None),
            P(),
            P("grp", None),
            P("grp", "seq", None),
            P("grp", "seq", None),
            P("grp"),
            P("grp"),
            P(("grp", "seq")),
        ),
        out_specs=P(("grp", "seq"), None),
        check_vma=False,
    )
```

```python
import jax
import jax.numpy as jnp
from jax import lax
from jax.experimental import pallas as pl
from jax.experimental.pallas import tpu as pltpu
from jax.sharding import PartitionSpec as P

MESH = pl.DeviceIdType.MESH
HEADS = 8
PANEL = 32
ROWS = 256
D = 1024
HD = 128
eps = 1e-06
SCALE = HD**-0.5
EVENT_AT = (0, 1, 2, 3, 4, 5, 12, 13, 6, 7, 8, 9, 10, 11, 14, 15)
ROW_AT = (4, 5, 0, 1, 2, 3, 12, 13, 6, 7, 8, 9, 10, 11, 14, 15)
NT = (((1,), (1,)), ((), ()))
BF = jnp.bfloat16
F32 = jnp.float32


def silu(z):
    h = z * 0.5
    return h + h * jnp.tanh(h)


def weight(s):
    h = (s * (0.5 * SCALE)).astype(BF)
    return h + h * jnp.tanh(h)


def layer_norm(x):
    mean = jnp.mean(x, axis=-1, keepdims=True)
    var = jnp.mean((x - mean) ** 2, axis=-1, keepdims=True)
    return (x - mean) / jnp.sqrt(var + eps)


def kernel(
    x_hbm,
    win_hbm,
    wout_hbm,
    hk_hbm,
    hv_hbm,
    hlen_hbm,
    cnt_hbm,
    pmap_hbm,
    out_ref,
    hlen_ref,
    cnt_ref,
    pmap_ref,
    x_v,
    n_v,
    win_v,
    hv_v,
    own_v,
    self_v,
    k_all,
    v_all,
    q_all,
    acc,
    osend,
    attn_v,
    wout_v,
    loc,
    k_snd,
    k_rcv,
    v_snd,
    v_rcv,
    q_snd,
    q_rcv,
    a_snd,
    a_rcv,
    w_snd,
    w_rcv,
):
    g = lax.axis_index("grp")
    s = lax.axis_index("seq")
    x, z, c = s // 8, (s // 2) % 4, s % 2
    xb, zb = x // 2, z // 2
    xh, zh = x + xb * (3 - 2 * x), z + zb * (3 - 2 * z)
    head = xh * 4 + zh * 2 + c

    def seq_of(x_, z_, c_):
        return x_ * 8 + z_ * 2 + c_

    def device(d, xb_, zb_):
        d2, d1, d0 = d // 4, (d // 2) % 2, d % 2
        xp = xh + d2 * (1 - 2 * xh)
        zp = zh + d1 * (1 - 2 * zh)
        cp = c + d0 * (1 - 2 * c)
        return (g, seq_of(xp + xb_ * (3 - 2 * xp), zp + zb_ * (3 - 2 * zp), cp)), xp * 4 + zp * 2 + cp

    def peer(d):
        return device(d, xb, zb)

    def across(d, core):
        return device(d, xb + (1 - core) * (1 - 2 * xb), zb + core * (1 - 2 * zb))

    row_partner = across(0, c)[0]
    event_partner = across(0, 1 - c)[0]

    def cols(h):
        return pl.ds(pl.multiple_of(h * HD, HD), HD)

    def block(i):
        return pl.ds(i * ROWS if isinstance(i, int) else pl.multiple_of(i * ROWS, ROWS), ROWS)

    def group(i):
        return pl.ds(i * 2 * ROWS if isinstance(i, int) else pl.multiple_of(i * 2 * ROWS, 2 * ROWS), 2 * ROWS)

    def ev(d):
        return block(EVENT_AT[d])

    def qs(d):
        return block(ROW_AT[d])

    def remote(src, dst, snd, rcv, dev):
        return pltpu.make_async_remote_copy(
            src_ref=src, dst_ref=dst, send_sem=snd, recv_sem=rcv, device_id=dev, device_id_type=MESH
        )

    barrier = pltpu.get_barrier_semaphore()
    partners = [peer(d)[0] for d in range(1, 8)] + [row_partner, event_partner]
    partners += [((g + d) % 4, s) for d in range(1, 4)]
    for dev in partners:
        pl.semaphore_signal(barrier, inc=1, device_id=dev, device_id_type=MESH)

    loads = [
        pltpu.make_async_copy(src, dst, loc.at[i])
        for i, (src, dst) in enumerate(
            [(x_hbm, x_v), (hlen_hbm, hlen_ref), (hv_hbm.at[0], hv_v)]
            + [(win_hbm.at[:, pl.ds(part * D, D)], win_v.at[part]) for part in (2, 3, 1, 0)]
            + [
                (wout_hbm, wout_v.at[block(g)]),
                (hk_hbm.at[0, :, cols(head)], k_all.at[ev(0)]),
                (cnt_hbm, cnt_ref),
                (pmap_hbm, pmap_ref),
            ]
        )
    ]
    for i in (1, 2, 0, 3):
        loads[i].start()

    loads[1].wait()
    loads[2].wait()
    pos = s * ROWS + lax.broadcasted_iota(jnp.int32, (ROWS, D), 0)
    hv_v[...] = jnp.where(pos < hlen_ref[0], hv_v[...].astype(F32), 0.0).astype(BF)
    v_all[ev(0), :] = hv_v[:, cols(head)]
    loads[0].wait()
    n_v[...] = layer_norm(x_v[...].astype(F32)).astype(BF)
    pl.semaphore_wait(barrier, len(partners))

    sends = []

    def go(copy):
        copy().start()
        sends.append(copy)

    def send_k(d):
        dev, h = peer(d)
        go(lambda: remote(hk_hbm.at[0, :, cols(h)], k_all.at[ev(d)], k_snd.at[d], k_rcv.at[d], dev))

    def send_v(d):
        dev, h = peer(d)
        go(lambda: remote(hv_v.at[:, cols(h)], v_all.at[ev(d)], v_snd.at[d], v_rcv.at[d], dev))

    q_own = own_v.at[2]

    def send_q(d):
        dev, h = peer(d)
        go(lambda: remote(q_own.at[:, cols(h)], q_all.at[qs(d)], q_snd.at[d], q_rcv.at[d], dev))

    def arrived(buf, rows, rcv, d):
        remote(buf.at[rows], buf.at[rows], rcv.at[d], rcv.at[d], event_partner).wait_recv()

    def await_kv(d):
        arrived(k_all, ev(d), k_rcv, d)
        arrived(v_all, ev(d), v_rcv, d)

    def await_q(d):
        arrived(q_all, qs(d), q_rcv, d)

    def pass_k(d):
        if d:
            arrived(k_all, ev(d), k_rcv, d)
        k_src = k_all.at[ev(d)] if d else hk_hbm.at[0, :, cols(head)]
        go(lambda: remote(k_src, k_all.at[ev(8 + d)], k_snd.at[8 + d], k_rcv.at[8 + d], event_partner))

    def pass_v(d):
        if d:
            arrived(v_all, ev(d), v_rcv, d)
        go(lambda: remote(v_all.at[ev(d)], v_all.at[ev(8 + d)], v_snd.at[8 + d], v_rcv.at[8 + d], event_partner))

    def pass_kv(d):
        pass_k(d)
        pass_v(d)

    def pass_q(d):
        if d:
            await_q(d)
        go(lambda: remote(q_all.at[qs(d)], q_all.at[qs(8 + d)], q_snd.at[8 + d], q_rcv.at[8 + d], row_partner))

    def w_rows(d, core):
        return pl.ds(pl.multiple_of(((g - d + 4) % 4) * 256 + core * 128, 128), 128)

    half = pl.ds(pl.multiple_of(c * 128, 128), 128)

    def send_w(d):
        dst = wout_v.at[w_rows(0, c)]
        go(lambda: remote(wout_hbm.at[half], dst, w_snd.at[d], w_rcv.at[d], ((g + d) % 4, s)))

    def pass_w(d):
        arrived(wout_v, w_rows(d, c), w_rcv, d)
        rows = wout_v.at[w_rows(d, c)]
        go(lambda: remote(rows, rows, w_snd.at[4 + d], w_rcv.at[4 + d], peer(1)[0]))

    near = (2, 4, 3, 5)
    for d in near:
        send_k(d)
    send_k(1)
    pass_k(0)

    for d in near:
        send_v(d)
    send_v(1)
    pass_v(0)

    for i in (4, 5, 6, 7, 8, 9, 10):
        loads[i].start()
    loads[3].wait()
    own_v[2] = silu(jnp.dot(n_v[...], win_v[2], preferred_element_type=F32)).astype(BF)
    q_all[qs(0), :] = own_v[2, :, cols(head)]
    send_q(1)
    pass_q(0)
    for d in near:
        send_q(d)
    for d in (6, 7):
        send_k(d)
        send_v(d)
    for d in (6, 7):
        send_q(d)
    for d in range(1, 4):
        send_w(d)

    pass_kv(1)
    pass_q(1)
    for load in loads[4:7]:
        load.wait()

    def rest(i, _):
        part = (2 - i) % 3 + (2 - i) // 2
        ds = pl.ds(0, D)
        own_v[part, :, ds] = silu(jnp.dot(n_v[...], win_v[part], preferred_element_type=F32)).astype(BF)
        return 0

    lax.fori_loop(0, 2, rest, 0)
    for d in near:
        pass_k(d)
    lax.fori_loop(2, 3, rest, 0)
    for h in range(HEADS):
        ds = pl.ds(h * HD, HD)
        dot = jnp.sum(own_v[2, :, ds].astype(F32) * own_v[3, :, ds].astype(F32), axis=-1, keepdims=True)
        self_v[:, ds] = silu(dot * SCALE).astype(BF).astype(F32) * own_v[1, :, ds].astype(F32)
    for d in near:
        pass_v(d)

    def attend(rows, events):
        sc = lax.dot_general(q_all[rows, :], k_all[events, :], NT, preferred_element_type=F32)
        return jnp.dot(weight(sc), v_all[events, :], preferred_element_type=F32)

    loads[8].wait()

    def early(n, _):
        @pl.when(n == 1)
        def _():
            await_q(8)
            await_q(9)

        @pl.when(n == 2)
        def _():
            for d in near:
                pass_q(d)

        @pl.when(n == 4)
        def _():
            for d in range(8, 14):
                await_kv(d)

        @pl.when(n == 5)
        def _():
            pass_kv(6)
            pass_kv(7)

        gr = (n + 2 - 2 * (n // 4)) % 4
        hf = n // 4
        events = pl.ds(pl.multiple_of(hf * 6 * ROWS, 6 * ROWS), 6 * ROWS)
        acc[hf, group(gr), :] = attend(group(gr), events)
        return 0

    lax.fori_loop(0, 6, early, 0)

    def partner_rows(m, _):
        @pl.when(m == 0)
        def _():
            await_q(10)
            await_q(11)

        @pl.when(m == 1)
        def _():
            pass_q(6)
            pass_q(7)
            await_q(12)
            await_q(13)

        acc[0, group(4 + m), :] = attend(group(4 + m), pl.ds(0, 12 * ROWS))
        acc[1, group(4 + m), :] = jnp.zeros((2 * ROWS, HD), F32)
        return 0

    lax.fori_loop(0, 2, partner_rows, 0)

    for d in range(1, 4):
        pass_w(d)

    def a_copy(d):
        if d < 8:
            dev = peer(d)[0]
        else:
            dev = across(d - 8, c)[0]
        return remote(osend.at[qs(d)], attn_v.at[d // 8, :, cols(head)], a_snd.at[d], a_rcv.at[d], dev)

    def send_sums(d):
        go(lambda: a_copy(d))

    for d in (14, 15):
        await_kv(d)
    late = pl.ds(12 * ROWS, 4 * ROWS)

    def finish(m, _):
        rows = pl.ds(pl.multiple_of((1 - m) * 8 * ROWS, 8 * ROWS), 4 * ROWS)
        osend[rows, :] = (acc[0, rows, :] + acc[1, rows, :] + attend(rows, late)).astype(BF)
        for i, ds in enumerate(((10, 11, 12, 13), (2, 3, 4, 5))):

            @pl.when(m == i)
            def _():
                for d in ds:
                    send_sums(d)

        return 0

    lax.fori_loop(0, 2, finish, 0)

    def whole(m, _):
        osend[group(7 - m), :] = attend(group(7 - m), pl.ds(0, 16 * ROWS)).astype(BF)
        for i, ds in enumerate(((14, 15), (6, 7))):

            @pl.when(m == i)
            def _():
                for d in ds:
                    send_sums(d)

        return 0

    await_q(14)
    await_q(15)
    lax.fori_loop(0, 2, whole, 0)

    def near_rows(m, _):
        gr = 3 - m
        osend[group(gr), :] = (acc[0, group(gr), :] + attend(group(gr), pl.ds(6 * ROWS, 10 * ROWS))).astype(BF)
        for i, ds in enumerate(((8, 9), (1,))):

            @pl.when(m == i)
            def _():
                for d in ds:
                    send_sums(d)

        return 0

    lax.fori_loop(0, 2, near_rows, 0)
    attn_v[0, :, cols(head)] = osend[qs(0), :]

    for d in range(1, 4):
        arrived(wout_v, w_rows(d, 1 - c), w_rcv, 4 + d)
    loads[7].wait()
    loads[9].wait()
    loads[10].wait()
    for d in range(1, 16):
        h = peer(d % 8)[1]
        remote(osend.at[qs(d)], attn_v.at[d // 8, :, cols(h)], a_snd.at[d], a_rcv.at[d], event_partner).wait_recv()

    attn = attn_v[0].astype(F32) + attn_v[1].astype(F32) + self_v[...]
    n_v[...] = (layer_norm(attn) * own_v[0].astype(F32)).astype(BF)

    mixed = x_v[...].astype(F32) + jnp.dot(n_v[...], wout_v[...], preferred_element_type=F32)
    for i in range(ROWS // PANEL):
        number = pmap_ref[i] * PANEL + lax.broadcasted_iota(jnp.int32, (PANEL, D), 0)
        keep = mixed[i * PANEL : (i + 1) * PANEL]
        out_ref[pl.ds(i * PANEL, PANEL), :] = jnp.where(number < cnt_ref[0], keep, 0.0).astype(BF)

    for copy in sends:
        copy().wait_send()


def per_device(cand_x, w_in, w_out, hist_keys, hist_values, hist_len, cand_count, panel_map):
    dma = pltpu.SemaphoreType.DMA
    return pl.pallas_call(
        kernel,
        out_shape=pltpu.VMEM((ROWS, D), BF),
        in_specs=[pl.BlockSpec(memory_space=pltpu.HBM)] * 8,
        out_specs=pl.BlockSpec(memory_space=pltpu.VMEM),
        scratch_shapes=[
            pltpu.SMEM((1,), jnp.int32),
            pltpu.SMEM((1,), jnp.int32),
            pltpu.SMEM((ROWS // PANEL,), jnp.int32),
            pltpu.VMEM((ROWS, D), BF),
            pltpu.VMEM((ROWS, D), BF),
            pltpu.VMEM((4, D, D), BF),
            pltpu.VMEM((ROWS, D), BF),
            pltpu.VMEM((4, ROWS, D), BF),
            pltpu.VMEM((ROWS, D), F32),
            pltpu.VMEM((16 * ROWS, HD), BF),
            pltpu.VMEM((16 * ROWS, HD), BF),
            pltpu.VMEM((16 * ROWS, HD), BF),
            pltpu.VMEM((2, 12 * ROWS, HD), F32),
            pltpu.VMEM((16 * ROWS, HD), BF),
            pltpu.VMEM((2, ROWS, D), BF),
            pltpu.VMEM((D, D), BF),
            dma((11,)),
            dma((16,)),
            dma((16,)),
            dma((16,)),
            dma((16,)),
            dma((16,)),
            dma((16,)),
            dma((16,)),
            dma((16,)),
            dma((8,)),
            dma((8,)),
        ],
        compiler_params=pltpu.CompilerParams(
            collective_id=0, has_side_effects=True, vmem_limit_bytes=56 * 2**20
        ),
    )(cand_x, w_in, w_out, hist_keys, hist_values, hist_len, cand_count, panel_map)


def solution(mesh):
    return jax.shard_map(
        per_device,
        mesh=mesh,
        in_specs=(
            P(("grp", "seq"), None),
            P(),
            P("grp", None),
            P("grp", "seq", None),
            P("grp", "seq", None),
            P("grp"),
            P("grp"),
            P(("grp", "seq")),
        ),
        out_specs=P(("grp", "seq"), None),
        check_vma=False,
    )
```

```python
import jax
import jax.numpy as jnp
from jax import lax
from jax.experimental import pallas as pl
from jax.experimental.pallas import tpu as pltpu
from jax.sharding import PartitionSpec as P

MESH = pl.DeviceIdType.MESH
HEADS = 8
PANEL = 32
ROWS = 256
D = 1024
HD = 128
eps = 1e-06
SCALE = HD**-0.5
EVENT_AT = (0, 1, 2, 3, 4, 5, 12, 13, 6, 7, 8, 9, 10, 11, 14, 15)
ROW_AT = (4, 5, 0, 1, 2, 3, 12, 13, 6, 7, 8, 9, 10, 11, 14, 15)
NT = (((1,), (1,)), ((), ()))
BF = jnp.bfloat16
F32 = jnp.float32


def silu(z):
    h = z * 0.5
    return h + h * jnp.tanh(h)


def weight(s):
    h = (s * (0.5 * SCALE)).astype(BF)
    return h + h * jnp.tanh(h)


def layer_norm(x):
    mean = jnp.mean(x, axis=-1, keepdims=True)
    var = jnp.mean((x - mean) ** 2, axis=-1, keepdims=True)
    return (x - mean) / jnp.sqrt(var + eps)


def kernel(
    x_hbm,
    win_hbm,
    wout_hbm,
    hk_hbm,
    hv_hbm,
    hlen_hbm,
    cnt_hbm,
    pmap_hbm,
    out_ref,
    hlen_ref,
    cnt_ref,
    pmap_ref,
    x_v,
    n_v,
    win_v,
    hv_v,
    own_v,
    self_v,
    k_all,
    v_all,
    q_all,
    acc,
    osend,
    attn_v,
    wout_v,
    loc,
    k_snd,
    k_rcv,
    v_snd,
    v_rcv,
    q_snd,
    q_rcv,
    a_snd,
    a_rcv,
    w_snd,
    w_rcv,
):
    g = lax.axis_index("grp")
    s = lax.axis_index("seq")
    x, z, c = s // 8, (s // 2) % 4, s % 2
    xb, zb = x // 2, z // 2
    xh, zh = x + xb * (3 - 2 * x), z + zb * (3 - 2 * z)
    head = xh * 4 + zh * 2 + c

    def seq_of(x_, z_, c_):
        return x_ * 8 + z_ * 2 + c_

    def device(d, xb_, zb_):
        d2, d1, d0 = d // 4, (d // 2) % 2, d % 2
        xp = xh + d2 * (1 - 2 * xh)
        zp = zh + d1 * (1 - 2 * zh)
        cp = c + d0 * (1 - 2 * c)
        return (g, seq_of(xp + xb_ * (3 - 2 * xp), zp + zb_ * (3 - 2 * zp), cp)), xp * 4 + zp * 2 + cp

    def peer(d):
        return device(d, xb, zb)

    def across(d, core):
        return device(d, xb + (1 - core) * (1 - 2 * xb), zb + core * (1 - 2 * zb))

    row_partner = across(0, c)[0]
    event_partner = across(0, 1 - c)[0]

    def cols(h):
        return pl.ds(pl.multiple_of(h * HD, HD), HD)

    def block(i):
        return pl.ds(i * ROWS if isinstance(i, int) else pl.multiple_of(i * ROWS, ROWS), ROWS)

    def group(i):
        return pl.ds(i * 2 * ROWS if isinstance(i, int) else pl.multiple_of(i * 2 * ROWS, 2 * ROWS), 2 * ROWS)

    def ev(d):
        return block(EVENT_AT[d])

    def qs(d):
        return block(ROW_AT[d])

    def remote(src, dst, snd, rcv, dev):
        return pltpu.make_async_remote_copy(
            src_ref=src, dst_ref=dst, send_sem=snd, recv_sem=rcv, device_id=dev, device_id_type=MESH
        )

    barrier = pltpu.get_barrier_semaphore()
    partners = [peer(d)[0] for d in range(1, 8)] + [row_partner, event_partner]
    partners += [((g + d) % 4, s) for d in range(1, 4)]
    for dev in partners:
        pl.semaphore_signal(barrier, inc=1, device_id=dev, device_id_type=MESH)

    loads = [
        pltpu.make_async_copy(src, dst, loc.at[i])
        for i, (src, dst) in enumerate(
            [(x_hbm, x_v), (hlen_hbm, hlen_ref), (hv_hbm.at[0], hv_v)]
            + [(win_hbm.at[:, pl.ds(part * D, D)], win_v.at[part]) for part in (2, 3, 1, 0)]
            + [
                (wout_hbm, wout_v.at[block(g)]),
                (hk_hbm.at[0, :, cols(head)], k_all.at[ev(0)]),
                (cnt_hbm, cnt_ref),
                (pmap_hbm, pmap_ref),
            ]
        )
    ]
    for i in (1, 2, 0, 3):
        loads[i].start()

    loads[1].wait()
    loads[2].wait()
    pos = s * ROWS + lax.broadcasted_iota(jnp.int32, (ROWS, D), 0)
    hv_v[...] = jnp.where(pos < hlen_ref[0], hv_v[...].astype(F32), 0.0).astype(BF)
    v_all[ev(0), :] = hv_v[:, cols(head)]
    loads[0].wait()
    n_v[...] = layer_norm(x_v[...].astype(F32)).astype(BF)
    pl.semaphore_wait(barrier, len(partners))

    sends = []

    def go(copy):
        copy().start()
        sends.append(copy)

    def send_k(d):
        dev, h = peer(d)
        go(lambda: remote(hk_hbm.at[0, :, cols(h)], k_all.at[ev(d)], k_snd.at[d], k_rcv.at[d], dev))

    def send_v(d):
        dev, h = peer(d)
        go(lambda: remote(hv_v.at[:, cols(h)], v_all.at[ev(d)], v_snd.at[d], v_rcv.at[d], dev))

    q_own = own_v.at[2]

    def send_q(d):
        dev, h = peer(d)
        go(lambda: remote(q_own.at[:, cols(h)], q_all.at[qs(d)], q_snd.at[d], q_rcv.at[d], dev))

    def arrived(buf, rows, rcv, d):
        remote(buf.at[rows], buf.at[rows], rcv.at[d], rcv.at[d], event_partner).wait_recv()

    def await_kv(d):
        arrived(k_all, ev(d), k_rcv, d)
        arrived(v_all, ev(d), v_rcv, d)

    def await_q(d):
        arrived(q_all, qs(d), q_rcv, d)

    def pass_k(d):
        if d:
            arrived(k_all, ev(d), k_rcv, d)
        k_src = k_all.at[ev(d)] if d else hk_hbm.at[0, :, cols(head)]
        go(lambda: remote(k_src, k_all.at[ev(8 + d)], k_snd.at[8 + d], k_rcv.at[8 + d], event_partner))

    def pass_v(d):
        if d:
            arrived(v_all, ev(d), v_rcv, d)
        go(lambda: remote(v_all.at[ev(d)], v_all.at[ev(8 + d)], v_snd.at[8 + d], v_rcv.at[8 + d], event_partner))

    def pass_kv(d):
        pass_k(d)
        pass_v(d)

    def pass_q(d):
        if d:
            await_q(d)
        go(lambda: remote(q_all.at[qs(d)], q_all.at[qs(8 + d)], q_snd.at[8 + d], q_rcv.at[8 + d], row_partner))

    def w_rows(d, core):
        return pl.ds(pl.multiple_of(((g - d + 4) % 4) * 256 + core * 128, 128), 128)

    half = pl.ds(pl.multiple_of(c * 128, 128), 128)

    def send_w(d):
        dst = wout_v.at[w_rows(0, c)]
        go(lambda: remote(wout_hbm.at[half], dst, w_snd.at[d], w_rcv.at[d], ((g + d) % 4, s)))

    def pass_w(d):
        arrived(wout_v, w_rows(d, c), w_rcv, d)
        rows = wout_v.at[w_rows(d, c)]
        go(lambda: remote(rows, rows, w_snd.at[4 + d], w_rcv.at[4 + d], peer(1)[0]))

    near = (2, 4, 3, 5)
    for d in near:
        send_k(d)
    send_k(1)
    pass_k(0)

    for d in near:
        send_v(d)
    send_v(1)
    pass_v(0)

    for i in (4, 5, 6, 7, 8, 9, 10):
        loads[i].start()
    loads[3].wait()
    own_v[2] = silu(jnp.dot(n_v[...], win_v[2], preferred_element_type=F32)).astype(BF)
    q_all[qs(0), :] = own_v[2, :, cols(head)]
    send_q(1)
    pass_q(0)
    for d in near:
        send_q(d)
    for d in (6, 7):
        send_k(d)
        send_v(d)
    for d in (6, 7):
        send_q(d)
    for d in range(1, 4):
        send_w(d)

    pass_kv(1)
    pass_q(1)
    for load in loads[4:7]:
        load.wait()

    def rest(i, _):
        part = (2 - i) % 3 + (2 - i) // 2
        ds = pl.ds(0, D)
        own_v[part, :, ds] = silu(jnp.dot(n_v[...], win_v[part], preferred_element_type=F32)).astype(BF)
        return 0

    lax.fori_loop(0, 2, rest, 0)
    for d in near:
        pass_k(d)
    lax.fori_loop(2, 3, rest, 0)
    for h in range(HEADS):
        ds = pl.ds(h * HD, HD)
        dot = jnp.sum(own_v[2, :, ds].astype(F32) * own_v[3, :, ds].astype(F32), axis=-1, keepdims=True)
        self_v[:, ds] = silu(dot * SCALE).astype(BF).astype(F32) * own_v[1, :, ds].astype(F32)
    for d in near:
        pass_v(d)

    def attend(rows, events):
        sc = lax.dot_general(q_all[rows, :], k_all[events, :], NT, preferred_element_type=F32)
        return jnp.dot(weight(sc), v_all[events, :], preferred_element_type=F32)

    loads[8].wait()

    def early(n, _):
        @pl.when(n == 1)
        def _():
            await_q(8)
            await_q(9)

        @pl.when(n == 2)
        def _():
            for d in near:
                pass_q(d)

        @pl.when(n == 4)
        def _():
            for d in range(8, 14):
                await_kv(d)

        @pl.when(n == 5)
        def _():
            pass_kv(6)
            pass_kv(7)

        gr = (n + 2 - 2 * (n // 4)) % 4
        hf = n // 4
        events = pl.ds(pl.multiple_of(hf * 6 * ROWS, 6 * ROWS), 6 * ROWS)
        acc[hf, group(gr), :] = attend(group(gr), events)
        return 0

    lax.fori_loop(0, 6, early, 0)

    def partner_rows(m, _):
        @pl.when(m == 0)
        def _():
            await_q(10)
            await_q(11)

        @pl.when(m == 1)
        def _():
            pass_q(6)
            pass_q(7)
            await_q(12)
            await_q(13)

        acc[0, group(4 + m), :] = attend(group(4 + m), pl.ds(0, 12 * ROWS))
        acc[1, group(4 + m), :] = jnp.zeros((2 * ROWS, HD), F32)
        return 0

    lax.fori_loop(0, 2, partner_rows, 0)

    for d in range(1, 4):
        pass_w(d)

    def a_copy(d):
        if d < 8:
            dev = peer(d)[0]
        else:
            dev = across(d - 8, c)[0]
        return remote(osend.at[qs(d)], attn_v.at[d // 8, :, cols(head)], a_snd.at[d], a_rcv.at[d], dev)

    def send_sums(d):
        go(lambda: a_copy(d))

    for d in (14, 15):
        await_kv(d)
    late = pl.ds(12 * ROWS, 4 * ROWS)

    def finish(m, _):
        rows = pl.ds(pl.multiple_of((1 - m) * 8 * ROWS, 8 * ROWS), 4 * ROWS)
        osend[rows, :] = (acc[0, rows, :] + acc[1, rows, :] + attend(rows, late)).astype(BF)
        for i, ds in enumerate(((10, 11, 12, 13), (2, 3, 4, 5))):

            @pl.when(m == i)
            def _():
                for d in ds:
                    send_sums(d)

        return 0

    lax.fori_loop(0, 2, finish, 0)

    def whole(m, _):
        osend[group(7 - m), :] = attend(group(7 - m), pl.ds(0, 16 * ROWS)).astype(BF)
        for i, ds in enumerate(((14, 15), (6, 7))):

            @pl.when(m == i)
            def _():
                for d in ds:
                    send_sums(d)

        return 0

    await_q(14)
    await_q(15)
    lax.fori_loop(0, 2, whole, 0)

    def near_rows(m, _):
        gr = 3 - m
        osend[group(gr), :] = (acc[0, group(gr), :] + attend(group(gr), pl.ds(6 * ROWS, 10 * ROWS))).astype(BF)
        for i, ds in enumerate(((8, 9), (1,))):

            @pl.when(m == i)
            def _():
                for d in ds:
                    send_sums(d)

        return 0

    lax.fori_loop(0, 2, near_rows, 0)
    attn_v[0, :, cols(head)] = osend[qs(0), :]

    for d in range(1, 4):
        arrived(wout_v, w_rows(d, 1 - c), w_rcv, 4 + d)
    loads[7].wait()
    loads[9].wait()
    loads[10].wait()
    for d in range(1, 16):
        h = peer(d % 8)[1]
        remote(osend.at[qs(d)], attn_v.at[d // 8, :, cols(h)], a_snd.at[d], a_rcv.at[d], event_partner).wait_recv()

    for lo in range(0, ROWS, 128):
        rows = pl.ds(lo, 128)
        attn = attn_v[0, rows].astype(F32) + attn_v[1, rows].astype(F32) + self_v[rows]
        n_v[rows] = (layer_norm(attn) * own_v[0, rows].astype(F32)).astype(BF)
        mixed = x_v[rows].astype(F32) + jnp.dot(n_v[rows], wout_v[...], preferred_element_type=F32)
        for i in range(128 // PANEL):
            number = pmap_ref[lo // PANEL + i] * PANEL + lax.broadcasted_iota(jnp.int32, (PANEL, D), 0)
            keep = mixed[i * PANEL : (i + 1) * PANEL]
            out_ref[pl.ds(lo + i * PANEL, PANEL), :] = jnp.where(number < cnt_ref[0], keep, 0.0).astype(BF)

    for copy in sends:
        copy().wait_send()


def per_device(cand_x, w_in, w_out, hist_keys, hist_values, hist_len, cand_count, panel_map):
    dma = pltpu.SemaphoreType.DMA
    return pl.pallas_call(
        kernel,
        out_shape=pltpu.VMEM((ROWS, D), BF),
        in_specs=[pl.BlockSpec(memory_space=pltpu.HBM)] * 8,
        out_specs=pl.BlockSpec(memory_space=pltpu.VMEM),
        scratch_shapes=[
            pltpu.SMEM((1,), jnp.int32),
            pltpu.SMEM((1,), jnp.int32),
            pltpu.SMEM((ROWS // PANEL,), jnp.int32),
            pltpu.VMEM((ROWS, D), BF),
            pltpu.VMEM((ROWS, D), BF),
            pltpu.VMEM((4, D, D), BF),
            pltpu.VMEM((ROWS, D), BF),
            pltpu.VMEM((4, ROWS, D), BF),
            pltpu.VMEM((ROWS, D), F32),
            pltpu.VMEM((16 * ROWS, HD), BF),
            pltpu.VMEM((16 * ROWS, HD), BF),
            pltpu.VMEM((16 * ROWS, HD), BF),
            pltpu.VMEM((2, 12 * ROWS, HD), F32),
            pltpu.VMEM((16 * ROWS, HD), BF),
            pltpu.VMEM((2, ROWS, D), BF),
            pltpu.VMEM((D, D), BF),
            dma((11,)),
            dma((16,)),
            dma((16,)),
            dma((16,)),
            dma((16,)),
            dma((16,)),
            dma((16,)),
            dma((16,)),
            dma((16,)),
            dma((8,)),
            dma((8,)),
        ],
        compiler_params=pltpu.CompilerParams(
            collective_id=0, has_side_effects=True, vmem_limit_bytes=56 * 2**20
        ),
    )(cand_x, w_in, w_out, hist_keys, hist_values, hist_len, cand_count, panel_map)


def solution(mesh):
    return jax.shard_map(
        per_device,
        mesh=mesh,
        in_specs=(
            P(("grp", "seq"), None),
            P(),
            P("grp", None),
            P("grp", "seq", None),
            P("grp", "seq", None),
            P("grp"),
            P("grp"),
            P(("grp", "seq")),
        ),
        out_specs=P(("grp", "seq"), None),
        check_vma=False,
    )
```
